128 devices in a mesh: table: 16 (over y, x), ctx: 8 (over z, core).
Axes of the slice: x: 4, y: 4, z: 4, core: 2. Of those that a mesh axis runs over, the one named last changes fastest.
Arguments:
- base_embed: bfloat16 [16, 1024, 2048], P('table', 'ctx'), may hold values from -6 to 6
- ngram_ids: int32 [16, 1024], P('table', 'ctx'), may hold values from 0 to 65535, as said below
- ngram_table: bfloat16 [65536, 2048], P(('table', 'ctx')), may hold values from -6 to 6
- embed_cot: bfloat16 [16, 1024, 2048], P('table', 'ctx'), may hold values from -6 to 6
- norm_gain: bfloat16 [2048], replicated, may hold values from 0.099609375 to 1.8984375
- w_qkv: bfloat16 [2048, 3072], replicated
Outputs:
- context: bfloat16 [16, 1024, 1024], P('table', 'ctx')
- table_grad: float32 [65536, 2048], P(('table', 'ctx'))
The draws below stay inside these ranges and needn't reach their ends.
Inputs may be any that keep to these rules, and one draw needn't show every extreme that they name: `ngram_ids`: device o of the joined table and ctx axes holds rows o * 512 to (o + 1) * 512 - 1. In each device's block of 128 tokens at most 4 tokens name rows of one owner, and exactly 4 name rows of some owner.
All inputs are finite; a program needn't handle non-finite values.
Results may differ from the reference program's by a relative error of at most 0.0085.
The reference program's roundings to bfloat16 on the way (of `rows`, `normed` and `weights`) count: a program that leaves them out, or rounds other values in their place, can miss the bound.
Values may be sent and summed in bfloat16 or wider, within the bound.
No kernel may reach another device: no remote copies, remote signals or barrier semaphores. Data moves between devices by JAX's collectives and lax.ppermute only.
A program may use at most 128 MiB of HBM per device.

```python
import jax
import jax.numpy as jnp
from jax import lax

D = 2048
HEAD = 128
HEADS = 8
TOK_DEV = 128
ROWS_DEV = 512
SEQS = 16
SEQ = 1024
OWNERS = 128
ROWS = 65536
CAP = 4
HD = 1024


def draw_ngram_ids(key, part):
    key = jax.random.fold_in(key, 11)
    key_common, key_blocks, key_local = jax.random.split(key, 3)
    blocks = SEQS * (SEQ // TOK_DEV)
    slots = OWNERS * CAP
    common = jax.random.randint(key_common, (), 0, OWNERS).astype(jnp.int32)
    owner_ids = jnp.arange(OWNERS, dtype=jnp.int32)
    slot_owner = jnp.arange(slots, dtype=jnp.int32) // CAP

    def one_block(block_key):
        key_pick, key_rank, key_order = jax.random.split(block_key, 3)
        picked = jax.random.permutation(key_pick, OWNERS)[:3].astype(jnp.int32)
        full = (owner_ids == common) | jnp.any(owner_ids[:, None] == picked[None, :], axis=1)
        ranks = jax.random.permutation(key_rank, slots).astype(jnp.int32)
        order_key = jnp.where(full[slot_owner], ranks - slots, ranks)
        chosen = jnp.argsort(order_key, stable=True)[:TOK_DEV]
        return jax.random.permutation(key_order, slot_owner[chosen]).astype(jnp.int32)
    owners = jax.vmap(one_block)(jax.random.split(key_blocks, blocks))
    local = jax.random.randint(key_local, (blocks, TOK_DEV), 0, ROWS_DEV).astype(jnp.int32)
    return (owners * ROWS_DEV + local).astype(jnp.int32).reshape(SEQS, SEQ)


def draw_w_qkv(key, part):
    key = jax.random.fold_in(key, 5)
    weights = jax.random.normal(key, (D, 3 * HD), jnp.float32) * D ** (-0.5)
    return weights.astype(jnp.bfloat16)


def shard_levels(own_key, dims, cuts, low, top_value):
    factor_of = 1.0
    for dim, blocks in cuts:
        steps = jax.random.uniform(jax.random.fold_in(jax.random.fold_in(own_key, 6), dim), (blocks,), jnp.float32, low / len(cuts), top_value / len(cuts))
        factor_of = factor_of * jnp.repeat(jnp.exp(steps), dims[dim] // blocks).reshape((-1,) + (1,) * (len(dims) - 1 - dim))
    return factor_of


def bell_draw(rng, extent, width, bound, pieces=(), kind=jnp.bfloat16):
    array = jax.random.normal(rng, extent, jnp.float32) * width
    if len(pieces) > 0:
        array = shard_levels(rng, extent, pieces, -0.22, 0.18) * array
    return jnp.clip(array, min=-bound, max=bound).astype(kind)


def setup_inputs(seed: int = 0) -> dict:
    arg_keys = jax.random.split(jax.random.key(seed), 7)
    return {
        "base_embed": bell_draw(arg_keys[0], (SEQS, SEQ, D), 1.0, 6.0, ((0, 16), (1, 8))),
        "ngram_ids": draw_ngram_ids(jax.random.fold_in(arg_keys[6], 71), 0),
        "ngram_table": bell_draw(arg_keys[2], (ROWS, D), 1.0, 6.0, ((0, 128),)),
        "embed_cot": bell_draw(arg_keys[3], (SEQS, SEQ, D), 1.0, 6.0, ((0, 16), (1, 8))),
        "norm_gain": jnp.clip(1.0 + 0.18 * jax.random.normal(arg_keys[4], (D,), jnp.float32), 0.099609375, 1.8984375).astype(jnp.bfloat16),
        "w_qkv": draw_w_qkv(jax.random.fold_in(arg_keys[6], 71), 0),
    }


def one_head(item):
    query, key, value = item
    scores = jnp.dot(query, key.T, preferred_element_type=jnp.float32) * HEAD ** (-0.5)
    positions = jnp.arange(SEQ, dtype=jnp.int32)
    allowed = positions[None, :] <= positions[:, None]
    top = lax.optimization_barrier(jnp.max(jnp.where(allowed, scores, -1e+30), axis=1))
    weights = jnp.where(allowed, jnp.exp(scores - top[:, None]), 0.0)
    total = lax.optimization_barrier(jnp.sum(weights, axis=1))
    mixed = jnp.dot(weights.astype(jnp.bfloat16), value, preferred_element_type=jnp.float32)
    return (mixed / total[:, None]).astype(jnp.bfloat16)

def reference(base_embed, ngram_ids, ngram_table, embed_cot, norm_gain, w_qkv):
    rows = ngram_table[ngram_ids]
    summed = base_embed.astype(jnp.float32) + rows.astype(jnp.float32)
    scale = lax.rsqrt(lax.optimization_barrier(jnp.mean(summed * summed, axis=-1, keepdims=True)) + 1e-05)
    normed = (summed * scale * norm_gain.astype(jnp.float32)).astype(jnp.bfloat16)
    projected = jnp.dot(normed.reshape(SEQS * SEQ, D), w_qkv, preferred_element_type=jnp.float32).astype(jnp.bfloat16)

    def split_heads(block):
        return block.reshape(SEQS, SEQ, HEADS, HEAD).transpose(0, 2, 1, 3).reshape(SEQS * HEADS, SEQ, HEAD)
    query = split_heads(projected[:, :HD])
    key = split_heads(projected[:, HD:2 * HD])
    value = split_heads(projected[:, 2 * HD:])
    mixed = lax.map(one_head, (query, key, value))
    context = mixed.reshape(SEQS, HEADS, SEQ, HEAD).transpose(0, 2, 1, 3).reshape(SEQS, SEQ, HD)
    table_grad = jnp.zeros((ROWS, D), jnp.float32).at[ngram_ids.reshape(-1)].add(embed_cot.reshape(SEQS * SEQ, D).astype(jnp.float32))
    return (context, table_grad)
```

```python
import functools

import jax
import jax.numpy as jnp
from jax import lax
from jax.experimental import pallas as pl
from jax.experimental.pallas import tpu as pltpu
from jax.sharding import PartitionSpec as P

HEAD = 128
HEADS = 8
CAP = 4
HALF = 1024
MB = 1024 * 1024


def iota(shape, dim):
    return lax.broadcasted_iota(jnp.int32, shape, dim)


def dot(a, b, dims=(((1,), (0,)), ((), ()))):
    return lax.dot_general(a, b, dims, preferred_element_type=jnp.float32)


def owner_grid(ids_ref, held):
    n = ids_ref.shape[1]
    ids = jnp.broadcast_to(ids_ref[...], (n, n))
    owner = ids // held
    return ids, owner, owner.astype(jnp.float32).T.astype(jnp.int32)


def pack_kernel(held, ids_ref, cot_ref, req_ref, send_ref):
    n = ids_ref.shape[1]
    ids, own_lane, own_sub = owner_grid(ids_ref, held)
    same = (own_lane == own_sub) & (iota((n, n), 0) < iota((n, n), 1))
    rank = jnp.sum(same.astype(jnp.int32), axis=0, keepdims=True)
    local = (ids - own_lane * held + 1).astype(jnp.float32)
    mine = own_lane == iota((n, n), 0)
    lane = iota((n, n), 1)
    req = jnp.zeros((n, n), jnp.float32)
    for c in range(CAP):
        found = jnp.sum(jnp.where(mine & (rank == c), local, 0.0), axis=1, keepdims=True)
        req = jnp.where(lane == c, found, req)
    req_ref[...] = req.astype(jnp.int32).reshape(n, 1, n)
    slot = own_lane[0:1] * (2 * CAP) + rank
    rows = iota((n * 2 * CAP, n), 0)
    low = (rows == slot).astype(jnp.bfloat16)
    high = (rows == slot + CAP).astype(jnp.bfloat16)
    send_ref[...] = (
        dot(low, cot_ref[:, :HALF]) + dot(high, cot_ref[:, HALF:])
    ).astype(jnp.bfloat16)


def slot_onehot(asked_ref, held):
    n = asked_ref.shape[0]
    wide = jnp.broadcast_to(asked_ref[...], (n, 2 * CAP, n)).reshape(n * 2 * CAP, n)
    rows = iota((n * 2 * CAP, n), 0) % (2 * CAP)
    lane = iota((n * 2 * CAP, n), 1)
    asked = jnp.sum(
        jnp.where(lane == rows % CAP, wide, 0).astype(jnp.float32), axis=1, keepdims=True
    ).astype(jnp.int32)
    hit = asked == iota((n * 2 * CAP, held), 1) + 1
    upper = iota((n * 2 * CAP, held), 0) % (2 * CAP) >= CAP
    low = jnp.where(hit & ~upper, 1.0, 0.0).astype(jnp.bfloat16)
    high = jnp.where(hit & upper, 1.0, 0.0).astype(jnp.bfloat16)
    return low, high


def rows_kernel(asked_ref, table_ref, send_ref):
    low, high = slot_onehot(asked_ref, table_ref.shape[0])
    send_ref[...] = (
        dot(low, table_ref[:, :HALF]) + dot(high, table_ref[:, HALF:])
    ).astype(jnp.bfloat16)


def grad_kernel(asked_ref, cot_ref, grad_ref):
    low, high = slot_onehot(asked_ref, grad_ref.shape[0])
    first = (((0,), (0,)), ((), ()))
    grad_ref[:, :HALF] = dot(low, cot_ref[...], first)
    grad_ref[:, HALF:] = dot(high, cot_ref[...], first)


def qkv_kernel(held, ids_ref, got_ref, base_ref, gain_ref, w_ref, out_ref, normed_ref):
    step = pl.program_id(0)

    @pl.when(step == 0)
    def _():
        n = ids_ref.shape[1]
        _, own_lane, own_sub = owner_grid(ids_ref, held)
        same = (own_lane == own_sub) & (iota((n, n), 1) < iota((n, n), 0))
        rank = jnp.sum(same.astype(jnp.int32), axis=1, keepdims=True)
        slot = own_sub[:, 0:1] * (2 * CAP) + rank
        rows = iota((n, n * 2 * CAP), 1)
        low = (rows == slot).astype(jnp.bfloat16)
        high = (rows == slot + CAP).astype(jnp.bfloat16)
        base = base_ref[...].astype(jnp.float32)
        sum_low = base[:, :HALF] + dot(low, got_ref[...])
        sum_high = base[:, HALF:] + dot(high, got_ref[...])
        square = jnp.sum(sum_low * sum_low, axis=1, keepdims=True) + jnp.sum(
            sum_high * sum_high, axis=1, keepdims=True
        )
        scale = lax.rsqrt(square * (1.0 / (2 * HALF)) + 1e-05)
        gain = gain_ref[...].astype(jnp.float32)
        normed_ref[:, :HALF] = (sum_low * scale * gain[:, :HALF]).astype(jnp.bfloat16)
        normed_ref[:, HALF:] = (sum_high * scale * gain[:, HALF:]).astype(jnp.bfloat16)

    heads = w_ref.shape[1] // HEAD
    made = dot(normed_ref[...], w_ref[...]).astype(jnp.bfloat16)
    for h in range(heads):
        out_ref[h] = made[:, h * HEAD : (h + 1) * HEAD]


def attention_kernel(block, qkv_ref, out_ref):
    seq = qkv_ref.shape[0]
    for i in range(seq // block):
        count = (i + 1) * block
        query = qkv_ref[i * block : count, :HEAD]
        keys = qkv_ref[:count, HEAD : 2 * HEAD]
        values = qkv_ref[:count, 2 * HEAD :]
        scores = dot(query, keys, (((1,), (1,)), ((), ()))) * HEAD ** (-0.5)
        allowed = iota((block, count), 1) <= iota((block, count), 0) + i * block
        scores = jnp.where(allowed, scores, -1e30)
        top = jnp.max(scores, axis=1, keepdims=True)
        weights = jnp.where(allowed, jnp.exp(scores - top), 0.0)
        total = jnp.sum(weights, axis=1, keepdims=True)
        mixed = dot(weights.astype(jnp.bfloat16), values)
        out_ref[i * block : count, :] = (mixed / total).astype(jnp.bfloat16)


def vmem(mb):
    return pltpu.CompilerParams(vmem_limit_bytes=mb * MB)


def cost(flops, moved):
    return pl.CostEstimate(flops=flops, bytes_accessed=moved, transcendentals=0)


def shards(base_embed, ngram_ids, ngram_table, embed_cot, norm_gain, w_qkv):
    tokens = ngram_ids.shape[1]
    width = base_embed.shape[2]
    held = ngram_table.shape[0]
    both = ("table", "ctx")
    owners = lax.axis_size("table") * lax.axis_size("ctx")
    ctx = lax.axis_size("ctx")
    slots = owners * 2 * CAP

    def exchange(x, axes=both):
        return lax.all_to_all(x, axes, split_axis=0, concat_axis=0, tiled=True)

    bf16, f32 = jnp.bfloat16, jnp.float32
    requests, cot_slots = pl.pallas_call(
        functools.partial(pack_kernel, held),
        out_shape=[
            jax.ShapeDtypeStruct((owners, 1, tokens), jnp.int32),
            jax.ShapeDtypeStruct((slots, HALF), bf16),
        ],
        compiler_params=vmem(24),
        cost_estimate=cost(2 * slots * tokens * width, 3 * MB),
        name="pack",
    )(ngram_ids, embed_cot[0])
    asked = exchange(requests)
    cot_all = exchange(cot_slots)
    row_slots = pl.pallas_call(
        rows_kernel,
        out_shape=jax.ShapeDtypeStruct((slots, HALF), bf16),
        compiler_params=vmem(24),
        cost_estimate=cost(2 * slots * held * width, 4 * MB),
        name="rows",
    )(asked, ngram_table)
    got = exchange(row_slots)
    table_grad = pl.pallas_call(
        grad_kernel,
        out_shape=jax.ShapeDtypeStruct((held, width), f32),
        compiler_params=vmem(24),
        cost_estimate=cost(2 * slots * held * width, 6 * MB),
        name="grad",
    )(asked, cot_all)
    columns = w_qkv.shape[1]
    blocks = 3 * 2
    per = columns // blocks
    heads_per = per // HEAD
    whole = lambda i: (0, 0)
    qkv = pl.pallas_call(
        functools.partial(qkv_kernel, held),
        grid=(blocks,),
        in_specs=[
            pl.BlockSpec((1, tokens), whole),
            pl.BlockSpec((slots, HALF), whole),
            pl.BlockSpec((tokens, width), whole),
            pl.BlockSpec((1, width), whole),
            pl.BlockSpec((width, per), lambda i: (0, i)),
        ],
        out_specs=pl.BlockSpec((heads_per, tokens, HEAD), lambda i: (i % 2, 0, i // 2)),
        out_shape=jax.ShapeDtypeStruct((ctx, tokens, 3 * HEAD), bf16),
        scratch_shapes=[pltpu.VMEM((tokens, width), bf16)],
        compiler_params=vmem(24),
        cost_estimate=cost(2 * tokens * width * columns, 16 * MB),
        name="qkv",
    )(ngram_ids, got, base_embed[0], norm_gain.reshape(1, width), w_qkv)
    mine = exchange(qkv, "ctx").reshape(ctx * tokens, 3 * HEAD)
    mixed = pl.pallas_call(
        functools.partial(attention_kernel, 256),
        out_shape=jax.ShapeDtypeStruct((ctx * tokens, HEAD), bf16),
        compiler_params=vmem(24),
        cost_estimate=cost(4 * ctx * tokens * ctx * tokens * HEAD, 2 * MB),
        name="attention",
    )(mine)
    context = exchange(mixed.reshape(ctx, tokens, HEAD), "ctx")
    context = context.transpose(1, 0, 2).reshape(tokens, HEADS * HEAD)
    return (context[None], table_grad)


def solution(mesh):
    return jax.shard_map(
        shards,
        mesh=mesh,
        in_specs=(
            P("table", "ctx", None),
            P("table", "ctx"),
            P(("table", "ctx"), None),
            P("table", "ctx", None),
            P(),
            P(),
        ),
        out_specs=(P("table", "ctx", None), P(("table", "ctx"), None)),
        check_vma=False,
    )
```

```python
import functools

import jax
import jax.numpy as jnp
from jax import lax
from jax.experimental import pallas as pl
from jax.experimental.pallas import tpu as pltpu
from jax.sharding import PartitionSpec as P

HEAD = 128
HEADS = 8
CAP = 4
TILE = 2 * CAP
HALF = 1024
MB = 1024 * 1024
BOTH = ("table", "ctx")


def iota(shape, dim):
    return lax.broadcasted_iota(jnp.int32, shape, dim)


def dot(a, b, dims=(((1,), (0,)), ((), ()))):
    return lax.dot_general(a, b, dims, preferred_element_type=jnp.float32)


def onehot(mask):
    return jnp.where(mask, 1.0, 0.0).astype(jnp.bfloat16)


def owner_grid(ids, held):
    n = ids.shape[1]
    owner = jnp.broadcast_to(ids, (n, n)) // held
    return owner, owner.astype(jnp.float32).T.astype(jnp.int32)


def asked_rows(ids_ref, held):
    n, _, tokens = ids_ref.shape
    me = lax.axis_index("table") * lax.axis_size("ctx") + lax.axis_index("ctx")
    wide = jnp.broadcast_to(ids_ref[...], (n, TILE, tokens)).reshape(n * TILE, tokens)
    local = wide - me * held
    mine = (local >= 0) & (local < held)
    earlier = onehot(iota((tokens, tokens), 0) < iota((tokens, tokens), 1))
    rank = dot(onehot(mine), earlier)
    slot = (iota(wide.shape, 0) % CAP).astype(jnp.float32)
    return jnp.where(mine & (rank == slot), local + 1, 0)


def rows_kernel(ids_ref, table_ref, send_ref):
    held = table_ref.shape[0]
    asked = asked_rows(ids_ref, held)
    row = jnp.sum(asked.astype(jnp.float32), axis=1, keepdims=True).astype(jnp.int32)
    shape = (row.shape[0], held)
    hit = row == iota(shape, 1) + 1
    upper = iota(shape, 0) % TILE >= CAP
    send_ref[...] = (
        dot(onehot(hit & ~upper), table_ref[:, :HALF])
        + dot(onehot(hit & upper), table_ref[:, HALF:])
    ).astype(jnp.bfloat16)


def cot_kernel(held, ids_ref, cot_ref, send_ref):
    ctx = lax.axis_size("ctx")
    tokens = ids_ref.shape[2]
    rows = send_ref.shape[0] * TILE
    first = lax.axis_index("table") * ctx
    for src in range(ctx):
        own_lane, own_sub = owner_grid(ids_ref[first + src], held)
        earlier = iota((tokens, tokens), 0) < iota((tokens, tokens), 1)
        same = jnp.where((own_lane == own_sub) & earlier, 1, 0)
        rank = jnp.sum(same, axis=0, keepdims=True)
        owner = own_lane[0:1]
        slot = jnp.where(owner % ctx == lax.axis_index("ctx"), owner // ctx * TILE + rank, -TILE)
        at = iota((rows, tokens), 0)
        cot = cot_ref.at[src * tokens : (src + 1) * tokens]
        made = dot(onehot(at == slot), cot[:, :HALF]) + dot(onehot(at == slot + CAP), cot[:, HALF:])
        send_ref[:, src * TILE : (src + 1) * TILE, :] = made.astype(jnp.bfloat16).reshape(
            rows // TILE, TILE, HALF
        )


def grad_kernel(ids_ref, cot_ref, grad_ref, low_ref, high_ref):
    held = grad_ref.shape[0]
    step = pl.program_id(0)
    half = pl.num_programs(0) // 2

    @pl.when(step == 0)
    def _():
        asked = asked_rows(ids_ref, held)
        lanes = (((1,), (1,)), ((), ()))
        ones = jnp.ones((8, asked.shape[1]), jnp.bfloat16)
        top = asked // 256
        row = 256.0 * dot(ones, top.astype(jnp.float32).astype(jnp.bfloat16), lanes) + dot(
            ones, (asked - top * 256).astype(jnp.float32).astype(jnp.bfloat16), lanes
        )
        shape = low_ref.shape
        hit = row[0:1].astype(jnp.int32) == iota(shape, 0) + 1
        upper = iota(shape, 1) % TILE >= CAP
        low_ref[...] = onehot(hit & ~upper)
        high_ref[...] = onehot(hit & upper)

    @pl.when(step < half)
    def _():
        grad_ref[...] = dot(low_ref[...], cot_ref[...])

    @pl.when(step >= half)
    def _():
        grad_ref[...] = dot(high_ref[...], cot_ref[...])


def qkv_kernel(held, ids_ref, got_ref, base_ref, gain_ref, w_hbm, *refs):
    out_refs, (w_ref, normed_ref, made_ref, sems) = refs[:HEADS], refs[HEADS:]
    blocks, _, per = w_ref.shape
    copies = [
        pltpu.make_async_copy(w_hbm.at[:, j * per : (j + 1) * per], w_ref.at[j], sems.at[j])
        for j in range(blocks)
    ]
    for copy in copies:
        copy.start()
    n = ids_ref.shape[1]
    own_lane, own_sub = owner_grid(ids_ref[...], held)
    same = (own_lane == own_sub) & (iota((n, n), 1) < iota((n, n), 0))
    rank = jnp.sum(jnp.where(same, 1, 0), axis=1, keepdims=True)
    slot = own_sub[:, 0:1] * TILE + rank
    at = iota((n, got_ref.shape[0]), 1)
    base = base_ref[...].astype(jnp.float32)
    low = base[:, :HALF] + dot(onehot(at == slot), got_ref[...])
    high = base[:, HALF:] + dot(onehot(at == slot + CAP), got_ref[...])
    square = jnp.sum(low * low, axis=1, keepdims=True) + jnp.sum(high * high, axis=1, keepdims=True)
    scale = lax.rsqrt(square * (1.0 / (2 * HALF)) + 1e-05)
    gain = gain_ref[...].astype(jnp.float32)
    normed_ref[:, :HALF] = (low * scale * gain[:, :HALF]).astype(jnp.bfloat16)
    normed_ref[:, HALF:] = (high * scale * gain[:, HALF:]).astype(jnp.bfloat16)
    for j, copy in enumerate(copies):
        copy.wait()
        made = dot(normed_ref[...], w_ref[j]).astype(jnp.bfloat16)
        for i in range(per // HEAD):
            kind, head = divmod(j * per // HEAD + i, HEADS)
            made_ref[head, :, kind * HEAD : (kind + 1) * HEAD] = made[:, i * HEAD : (i + 1) * HEAD]
    me = lax.axis_index("ctx")
    for shift, ref in enumerate(out_refs):
        ref[...] = made_ref[(me + shift) % HEADS]


def attention_kernel(block, *refs):
    ins, outs, (qkv_ref, mixed_ref) = refs[:HEADS], refs[HEADS : 2 * HEADS], refs[2 * HEADS :]
    tokens = ins[0].shape[0]
    seq = tokens * HEADS
    me = lax.axis_index("ctx")
    for shift, ref in enumerate(ins):
        source = (me + HEADS - shift) % HEADS
        qkv_ref[pl.ds(pl.multiple_of(source * tokens, tokens), tokens), :] = ref[...]
    for i in range(seq // block):
        count = (i + 1) * block
        query = qkv_ref[i * block : count, :HEAD]
        keys = qkv_ref[:count, HEAD : 2 * HEAD]
        values = qkv_ref[:count, 2 * HEAD :]
        scores = dot(query, keys, (((1,), (1,)), ((), ()))) * HEAD ** (-0.5)
        allowed = iota((block, count), 1) <= iota((block, count), 0) + i * block
        scores = jnp.where(allowed, scores, -1e30)
        top = jnp.max(scores, axis=1, keepdims=True)
        weights = jnp.where(allowed, jnp.exp(scores - top), 0.0)
        total = jnp.sum(weights, axis=1, keepdims=True)
        mixed = dot(weights.astype(jnp.bfloat16), values)
        mixed_ref[i * block : count, :] = (mixed / total).astype(jnp.bfloat16)
    for shift, ref in enumerate(outs):
        target = (me + shift) % HEADS
        ref[...] = mixed_ref[pl.ds(pl.multiple_of(target * tokens, tokens), tokens), :]


def join_kernel(*refs):
    ins, out_ref = refs[:HEADS], refs[HEADS]
    me = lax.axis_index("ctx")
    for shift, ref in enumerate(ins):
        head = (me + HEADS - shift) % HEADS
        out_ref[:, pl.ds(pl.multiple_of(head * HEAD, HEAD), HEAD)] = ref[...]


def call(kernel, out, flops, moved, mb=24, **kwargs):
    return pl.pallas_call(
        kernel,
        out_shape=out,
        compiler_params=pltpu.CompilerParams(vmem_limit_bytes=mb * MB),
        cost_estimate=pl.CostEstimate(flops=flops, bytes_accessed=moved, transcendentals=0),
        **kwargs,
    )


def exchange(x, axes):
    return lax.all_to_all(x, axes, split_axis=0, concat_axis=0, tiled=True)


def shift_all(pieces):
    n = len(pieces)
    moved = [
        lax.ppermute(pieces[k], "ctx", [(i, (i + k) % n) for i in range(n)]) for k in range(1, n)
    ]
    return [pieces[0], *moved]


def shards(base_embed, ngram_ids, ngram_table, embed_cot, norm_gain, w_qkv):
    tokens = ngram_ids.shape[1]
    width = base_embed.shape[2]
    held = ngram_table.shape[0]
    table = lax.axis_size("table")
    ctx = lax.axis_size("ctx")
    owners = table * ctx
    slots = owners * TILE
    columns = w_qkv.shape[1]
    bf16, f32 = jnp.bfloat16, jnp.float32
    shape = jax.ShapeDtypeStruct

    all_ids = exchange(jnp.broadcast_to(ngram_ids[None], (owners, 1, tokens)), BOTH)
    seq_cot = lax.all_gather(embed_cot[0], "ctx", axis=0, tiled=True)
    row_slots = call(
        rows_kernel,
        shape((slots, HALF), bf16),
        2 * slots * held * width,
        4 * MB,
        name="rows",
    )(all_ids, ngram_table)
    got = exchange(row_slots, BOTH)
    cot_slots = call(
        functools.partial(cot_kernel, held),
        shape((table, ctx * TILE, HALF), bf16),
        2 * slots * tokens * width,
        6 * MB,
        name="cot_slots",
    )(all_ids, seq_cot)
    cot_all = exchange(cot_slots, "table").reshape(slots, HALF)
    blocks = 4
    per = width // blocks
    table_grad = call(
        grad_kernel,
        shape((held, width), f32),
        2 * slots * held * width,
        6 * MB,
        name="grad",
        grid=(blocks,),
        in_specs=[
            pl.BlockSpec((owners, 1, tokens), lambda j: (0, 0, 0)),
            pl.BlockSpec((slots, per), lambda j: (0, j % 2)),
        ],
        out_specs=pl.BlockSpec((held, per), lambda j: (0, j)),
        scratch_shapes=[pltpu.VMEM((held, slots), bf16)] * 2,
    )(all_ids, cot_all)
    blocks = 6
    whole = pl.BlockSpec(memory_space=pltpu.VMEM)
    qkv = call(
        functools.partial(qkv_kernel, held),
        [shape((tokens, 3 * HEAD), bf16)] * HEADS,
        2 * tokens * width * columns,
        16 * MB,
        mb=32,
        name="qkv",
        in_specs=[whole] * 4 + [pl.BlockSpec(memory_space=pltpu.HBM)],
        scratch_shapes=[
            pltpu.VMEM((blocks, width, columns // blocks), bf16),
            pltpu.VMEM((tokens, width), bf16),
            pltpu.VMEM((HEADS, tokens, 3 * HEAD), bf16),
            pltpu.SemaphoreType.DMA((blocks,)),
        ],
    )(ngram_ids, got, base_embed[0], norm_gain.reshape(1, width), w_qkv)
    mixed = call(
        functools.partial(attention_kernel, 256),
        [shape((tokens, HEAD), bf16)] * HEADS,
        4 * ctx * tokens * ctx * tokens * HEAD,
        2 * MB,
        name="attention",
        scratch_shapes=[
            pltpu.VMEM((ctx * tokens, 3 * HEAD), bf16),
            pltpu.VMEM((ctx * tokens, HEAD), bf16),
        ],
    )(*shift_all(qkv))
    context = call(
        join_kernel, shape((tokens, HEADS * HEAD), bf16), 0, MB // 2, name="join"
    )(*shift_all(mixed))
    return (context[None], table_grad)


def solution(mesh):
    return jax.shard_map(
        shards,
        mesh=mesh,
        in_specs=(
            P("table", "ctx", None),
            P("table", "ctx"),
            P(("table", "ctx"), None),
            P("table", "ctx", None),
            P(),
            P(),
        ),
        out_specs=(P("table", "ctx", None), P(("table", "ctx"), None)),
        check_vma=False,
    )
```

```python
import functools

import jax
import jax.numpy as jnp
from jax import lax
from jax.experimental import pallas as pl
from jax.experimental.pallas import tpu as pltpu
from jax.sharding import PartitionSpec as P

HEAD = 128
HEADS = 8
CAP = 4
TILE = 2 * CAP
HALF = 1024
MB = 1024 * 1024
AHEAD = 3
BOTH = ("table", "ctx")


def iota(shape, dim):
    return lax.broadcasted_iota(jnp.int32, shape, dim)


def dot(a, b, dims=(((1,), (0,)), ((), ()))):
    return lax.dot_general(a, b, dims, preferred_element_type=jnp.float32)


def onehot(mask):
    return jnp.where(mask, 1.0, 0.0).astype(jnp.bfloat16)


def owner_grid(ids, held):
    n = ids.shape[1]
    owner = jnp.broadcast_to(ids, (n, n)) // held
    return owner, owner.astype(jnp.float32).T.astype(jnp.int32)


def asked_rows(ids_ref, held):
    n, _, tokens = ids_ref.shape
    me = lax.axis_index("table") * lax.axis_size("ctx") + lax.axis_index("ctx")
    wide = jnp.broadcast_to(ids_ref[...], (n, TILE, tokens)).reshape(n * TILE, tokens)
    local = wide - me * held
    mine = (local >= 0) & (local < held)
    earlier = onehot(iota((tokens, tokens), 0) < iota((tokens, tokens), 1))
    rank = dot(onehot(mine), earlier)
    slot = (iota(wide.shape, 0) % CAP).astype(jnp.float32)
    return jnp.where(mine & (rank == slot), local + 1, 0)


def pack_kernel(held, ids_ref, cot_ref, send_hbm, stage_ref, sem):
    tokens = ids_ref.shape[1]
    own_lane, own_sub = owner_grid(ids_ref[...], held)
    earlier = iota((tokens, tokens), 0) < iota((tokens, tokens), 1)
    rank = jnp.sum(jnp.where((own_lane == own_sub) & earlier, 1, 0), axis=0, keepdims=True)
    slot = own_lane[0:1] * TILE + rank
    at = iota((stage_ref.shape[0] * TILE, tokens), 0)
    made = dot(onehot(at == slot), cot_ref[:, :HALF]) + dot(onehot(at == slot + CAP), cot_ref[:, HALF:])
    stage_ref[...] = made.astype(jnp.bfloat16).reshape(stage_ref.shape)
    copy = pltpu.make_async_copy(stage_ref, send_hbm.at[:, 1], sem)
    copy.start()
    copy.wait()


def rows_kernel(ids_ref, table_ref, cot_hbm, send_hbm, stage_ref, sems):
    held = table_ref.shape[0]
    asked = asked_rows(ids_ref, held)
    row = jnp.sum(asked.astype(jnp.float32), axis=1, keepdims=True).astype(jnp.int32)
    parts = sems.shape[0]
    block = row.shape[0] // parts
    shape = (block, held)
    upper = iota(shape, 0) % TILE >= CAP
    copies = []
    for part in range(parts):
        hit = row[part * block : (part + 1) * block] == iota(shape, 1) + 1
        made = dot(onehot(hit & ~upper), table_ref[:, :HALF]) + dot(
            onehot(hit & upper), table_ref[:, HALF:]
        )
        at = pl.ds(part * (block // TILE), block // TILE)
        stage_ref[at] = made.astype(jnp.bfloat16).reshape(block // TILE, TILE, HALF)
        copies.append(
            pltpu.make_async_copy(stage_ref.at[at], send_hbm.at[at, 0], sems.at[part])
        )
        copies[-1].start()
    for copy in copies:
        copy.wait()


def prepare_kernel(ids_ref, gain_ref, low_ref, high_ref, wide_gain_ref):
    wide_gain_ref[...] = jnp.broadcast_to(gain_ref[...].astype(jnp.float32), wide_gain_ref.shape)
    asked = asked_rows(ids_ref, low_ref.shape[0])
    lanes = (((1,), (1,)), ((), ()))
    ones = jnp.ones((8, asked.shape[1]), jnp.bfloat16)
    top = asked // 256
    row = 256.0 * dot(ones, top.astype(jnp.float32).astype(jnp.bfloat16), lanes) + dot(
        ones, (asked - top * 256).astype(jnp.float32).astype(jnp.bfloat16), lanes
    )
    shape = low_ref.shape
    hit = row[0:1].astype(jnp.int32) == iota(shape, 0) + 1
    upper = iota(shape, 1) % TILE >= CAP
    low_ref[...] = onehot(hit & ~upper)
    high_ref[...] = onehot(hit & upper)


def grad_kernel(low_ref, high_ref, cot_ref, grad_ref):
    step = pl.program_id(0)
    cot = cot_ref[...].reshape(low_ref.shape[1], grad_ref.shape[1])

    @pl.when(step % 2 == 0)
    def _():
        grad_ref[...] = dot(low_ref[...], cot)

    @pl.when(step % 2 == 1)
    def _():
        grad_ref[...] = dot(high_ref[...], cot)


def qkv_kernel(
    held, ids_ref, got_hbm, base_ref, gain_ref, w_hbm, low_hbm, high_hbm, out_ref, got_ref, w_ref,
    normed_ref, sems,
):
    blocks, _, per = w_ref.shape
    load = pltpu.make_async_copy(got_hbm.at[:, 0], got_ref, sems.at[blocks])
    load.start()
    copies = [
        pltpu.make_async_copy(w_hbm.at[:, j * per : (j + 1) * per], w_ref.at[j], sems.at[j])
        for j in range(blocks)
    ]
    for copy in copies[:AHEAD]:
        copy.start()
    n = ids_ref.shape[1]
    slots = got_ref.shape[0] * TILE
    own_lane, own_sub = owner_grid(ids_ref[...], held)
    same = (own_lane == own_sub) & (iota((n, n), 1) < iota((n, n), 0))
    rank = jnp.sum(jnp.where(same, 1, 0), axis=1, keepdims=True)
    slot = own_sub[:, 0:1] * TILE + rank
    pick = onehot(iota((2 * n, slots), 1) == jnp.concatenate([slot, slot + CAP], axis=0))
    load.wait()
    rows = dot(pick, got_ref[...].reshape(slots, HALF))
    low = base_ref[:, :HALF].astype(jnp.float32) + rows[:n]
    high = base_ref[:, HALF:].astype(jnp.float32) + rows[n:]
    square = jnp.sum(low * low, axis=1, keepdims=True) + jnp.sum(high * high, axis=1, keepdims=True)
    scale = lax.rsqrt(square * (1.0 / (2 * HALF)) + 1e-05)
    gain = gain_ref[0:1]
    normed_ref[:, :HALF] = (low * scale * gain[:, :HALF]).astype(jnp.bfloat16)
    normed_ref[:, HALF:] = (high * scale * gain[:, HALF:]).astype(jnp.bfloat16)
    for j, copy in enumerate(copies):
        copy.wait()
        if j + AHEAD < blocks:
            copies[j + AHEAD].start()
        made = dot(normed_ref[...], w_ref[j]).astype(jnp.bfloat16)
        for i in range(per // HEAD):
            kind, head = divmod(j * per // HEAD + i, HEADS)
            out_ref[head, :, kind * HEAD : (kind + 1) * HEAD] = made[:, i * HEAD : (i + 1) * HEAD]


def spread_kernel(ids_ref, out_ref):
    out_ref[...] = jnp.broadcast_to(ids_ref[...][None], out_ref.shape)


def attention_kernel(block, qkv_ref, out_ref):
    seq = qkv_ref.shape[0]
    for i in range(seq // block):
        count = (i + 1) * block
        query = qkv_ref[i * block : count, :HEAD]
        keys = qkv_ref[:count, HEAD : 2 * HEAD]
        values = qkv_ref[:count, 2 * HEAD :]
        scores = dot(query, keys, (((1,), (1,)), ((), ()))) * HEAD ** (-0.5)
        allowed = iota((block, count), 1) <= iota((block, count), 0) + i * block
        scores = jnp.where(allowed, scores, -1e30)
        top = jnp.max(scores, axis=1, keepdims=True)
        weights = jnp.where(allowed, jnp.exp(scores - top), 0.0)
        total = jnp.sum(weights, axis=1, keepdims=True)
        mixed = dot(weights.astype(jnp.bfloat16), values)
        out_ref[i * block : count, :] = (mixed / total).astype(jnp.bfloat16)


def call(kernel, out, flops, moved, mb=24, **kwargs):
    return pl.pallas_call(
        kernel,
        out_shape=out,
        compiler_params=pltpu.CompilerParams(vmem_limit_bytes=mb * MB),
        cost_estimate=pl.CostEstimate(flops=flops, bytes_accessed=moved, transcendentals=0),
        **kwargs,
    )


def exchange(x, axes):
    return lax.all_to_all(x, axes, split_axis=0, concat_axis=0, tiled=True)


def shards(base_embed, ngram_ids, ngram_table, embed_cot, norm_gain, w_qkv):
    tokens = ngram_ids.shape[1]
    width = base_embed.shape[2]
    held = ngram_table.shape[0]
    table = lax.axis_size("table")
    ctx = lax.axis_size("ctx")
    owners = table * ctx
    slots = owners * TILE
    columns = w_qkv.shape[1]
    bf16, f32 = jnp.bfloat16, jnp.float32
    shape = jax.ShapeDtypeStruct
    whole = pl.BlockSpec(memory_space=pltpu.VMEM)
    remote = pl.BlockSpec(memory_space=pltpu.HBM)

    near_hbm = pltpu.with_memory_space_constraint(ngram_ids, pltpu.HBM)
    all_ids = exchange(
        call(spread_kernel, shape((owners, 1, tokens), jnp.int32), 0, 0, name="spread")(near_hbm), BOTH
    )
    blocks = pltpu.HBM((owners, 2, TILE, HALF), bf16)
    stage = pltpu.VMEM((owners, TILE, HALF), bf16)
    send = call(
        functools.partial(pack_kernel, held),
        blocks,
        2 * slots * tokens * width,
        3 * MB,
        name="pack",
        in_specs=[whole] * 2,
        out_specs=remote,
        scratch_shapes=[stage, pltpu.SemaphoreType.DMA],
    )(ngram_ids, embed_cot[0])
    send = call(
        rows_kernel,
        blocks,
        2 * slots * held * width,
        4 * MB,
        name="rows",
        in_specs=[whole, whole, remote],
        out_specs=remote,
        scratch_shapes=[stage, pltpu.SemaphoreType.DMA((4,))],
        input_output_aliases={2: 0},
    )(all_ids, ngram_table, send)
    got = exchange(send, BOTH)
    low, high, gain = call(
        prepare_kernel,
        [pltpu.VMEM((held, slots), bf16)] * 2 + [shape((8, width), f32)],
        20000 * MB,
        2 * MB,
        name="prepare",
    )(all_ids, norm_gain.reshape(1, width))
    w_blocks = 8
    qkv = call(
        functools.partial(qkv_kernel, held),
        shape((ctx, tokens, 3 * HEAD), bf16),
        2 * tokens * width * columns,
        16 * MB,
        name="qkv",
        in_specs=[whole, remote, whole, whole, remote, remote, remote],
        out_specs=whole,
        scratch_shapes=[
            stage,
            pltpu.VMEM((w_blocks, width, columns // w_blocks), bf16),
            pltpu.VMEM((tokens, width), bf16),
            pltpu.SemaphoreType.DMA((w_blocks + 1,)),
        ],
    )(
        ngram_ids,
        got,
        base_embed[0],
        gain,
        pltpu.with_memory_space_constraint(w_qkv, pltpu.HBM),
        low,
        high,
    )
    steps = 4
    per = width // steps
    table_grad = call(
        grad_kernel,
        shape((held, width), f32),
        2 * slots * held * width,
        6 * MB,
        name="grad",
        grid=(steps,),
        in_specs=[
            pl.BlockSpec((held, slots), lambda j: (0, 0)),
            pl.BlockSpec((held, slots), lambda j: (0, 0)),
            pl.BlockSpec((owners, None, TILE, per), lambda j: (0, 1, 0, j // 2)),
        ],
        out_specs=pl.BlockSpec((held, per), lambda j: (0, j % 2 * 2 + j // 2)),
    )(low, high, got)
    mine = exchange(qkv, "ctx").reshape(ctx * tokens, 3 * HEAD)
    mixed = call(
        functools.partial(attention_kernel, 256),
        shape((ctx * tokens, HEAD), bf16),
        4 * ctx * tokens * ctx * tokens * HEAD,
        2 * MB,
        name="attention",
    )(mine)
    context = exchange(mixed.reshape(ctx, tokens, HEAD), "ctx")
    context = context.transpose(1, 0, 2).reshape(tokens, HEADS * HEAD)
    return (context[None], table_grad)


def solution(mesh):
    return jax.shard_map(
        shards,
        mesh=mesh,
        in_specs=(
            P("table", "ctx", None),
            P("table", "ctx"),
            P(("table", "ctx"), None),
            P("table", "ctx", None),
            P(),
            P(),
        ),
        out_specs=(P("table", "ctx", None), P(("table", "ctx"), None)),
        check_vma=False,
    )
```

```python
import functools

import jax
import jax.numpy as jnp
from jax import lax
from jax.experimental import pallas as pl
from jax.experimental.pallas import tpu as pltpu
from jax.sharding import PartitionSpec as P

HEAD = 128
HEADS = 8
CAP = 4
TILE = 2 * CAP
HALF = 1024
MB = 1024 * 1024
AHEAD = 4
BOTH = ("table", "ctx")


def iota(shape, dim):
    return lax.broadcasted_iota(jnp.int32, shape, dim)


def dot(a, b, dims=(((1,), (0,)), ((), ()))):
    return lax.dot_general(a, b, dims, preferred_element_type=jnp.float32)


def onehot(mask):
    return jnp.where(mask, 1.0, 0.0).astype(jnp.bfloat16)


def owner_grid(ids, held):
    n = ids.shape[1]
    owner = jnp.broadcast_to(ids, (n, n)) // held
    return owner, owner.astype(jnp.float32).T.astype(jnp.int32)


def asked_rows(ids_ref, held):
    n, _, tokens = ids_ref.shape
    me = lax.axis_index("table") * lax.axis_size("ctx") + lax.axis_index("ctx")
    wide = jnp.broadcast_to(ids_ref[...], (n, TILE, tokens)).reshape(n * TILE, tokens)
    local = wide - me * held
    mine = (local >= 0) & (local < held)
    earlier = onehot(iota((tokens, tokens), 0) < iota((tokens, tokens), 1))
    rank = dot(onehot(mine), earlier)
    slot = (iota(wide.shape, 0) % CAP).astype(jnp.float32)
    return jnp.where(mine & (rank == slot), local + 1, 0)


def pack_kernel(held, ids_ref, cot_ref, send_hbm, stage_ref, sem):
    tokens = ids_ref.shape[1]
    own_lane, own_sub = owner_grid(ids_ref[...], held)
    earlier = iota((tokens, tokens), 0) < iota((tokens, tokens), 1)
    rank = jnp.sum(jnp.where((own_lane == own_sub) & earlier, 1, 0), axis=0, keepdims=True)
    slot = own_lane[0:1] * TILE + rank
    at = iota((stage_ref.shape[0] * TILE, tokens), 0)
    made = dot(onehot(at == slot), cot_ref[:, :HALF]) + dot(onehot(at == slot + CAP), cot_ref[:, HALF:])
    stage_ref[...] = made.astype(jnp.bfloat16).reshape(stage_ref.shape)
    copy = pltpu.make_async_copy(stage_ref, send_hbm.at[:, 1], sem)
    copy.start()
    copy.wait()


def rows_kernel(ids_ref, table_ref, cot_hbm, send_hbm, stage_ref, sems):
    held = table_ref.shape[0]
    asked = asked_rows(ids_ref, held)
    row = jnp.sum(asked.astype(jnp.float32), axis=1, keepdims=True).astype(jnp.int32)
    parts = sems.shape[0]
    block = row.shape[0] // parts
    shape = (block, held)
    upper = iota(shape, 0) % TILE >= CAP
    copies = []
    for part in range(parts):
        hit = row[part * block : (part + 1) * block] == iota(shape, 1) + 1
        made = dot(onehot(hit & ~upper), table_ref[:, :HALF]) + dot(
            onehot(hit & upper), table_ref[:, HALF:]
        )
        at = pl.ds(part * (block // TILE), block // TILE)
        stage_ref[at] = made.astype(jnp.bfloat16).reshape(block // TILE, TILE, HALF)
        copies.append(
            pltpu.make_async_copy(stage_ref.at[at], send_hbm.at[at, 0], sems.at[part])
        )
        copies[-1].start()
    for copy in copies:
        copy.wait()


def prepare_kernel(ids_ref, gain_ref, low_ref, high_ref, wide_gain_ref):
    wide_gain_ref[...] = jnp.broadcast_to(gain_ref[...].astype(jnp.float32), wide_gain_ref.shape)
    asked = asked_rows(ids_ref, low_ref.shape[0])
    lanes = (((1,), (1,)), ((), ()))
    ones = jnp.ones((8, asked.shape[1]), jnp.bfloat16)
    top = asked // 256
    row = 256.0 * dot(ones, top.astype(jnp.float32).astype(jnp.bfloat16), lanes) + dot(
        ones, (asked - top * 256).astype(jnp.float32).astype(jnp.bfloat16), lanes
    )
    shape = low_ref.shape
    hit = row[0:1].astype(jnp.int32) == iota(shape, 0) + 1
    upper = iota(shape, 1) % TILE >= CAP
    low_ref[...] = onehot(hit & ~upper)
    high_ref[...] = onehot(hit & upper)


def grad_kernel(low_ref, high_ref, cot_ref, grad_ref):
    step = pl.program_id(0)
    cot = cot_ref[...].reshape(low_ref.shape[1], grad_ref.shape[1])

    @pl.when(step % 2 == 0)
    def _():
        grad_ref[...] = dot(low_ref[...], cot)

    @pl.when(step % 2 == 1)
    def _():
        grad_ref[...] = dot(high_ref[...], cot)


def qkv_kernel(
    held, ids_ref, got_hbm, base_ref, gain_ref, w_hbm, low_hbm, high_hbm, *refs
):
    *out_refs, got_ref, w_ref, normed_ref, total_ref, made_ref, sems = refs
    blocks, depth, columns = w_ref.shape
    per = columns // 6
    load = pltpu.make_async_copy(got_hbm.at[:, 0], got_ref, sems.at[blocks])
    load.start()
    copies = [
        pltpu.make_async_copy(w_hbm.at[j * depth : (j + 1) * depth], w_ref.at[j], sems.at[j])
        for j in range(blocks)
    ]
    for copy in copies[:AHEAD]:
        copy.start()
    n = ids_ref.shape[1]
    slots = got_ref.shape[0] * TILE
    own_lane, own_sub = owner_grid(ids_ref[...], held)
    same = (own_lane == own_sub) & (iota((n, n), 1) < iota((n, n), 0))
    rank = jnp.sum(jnp.where(same, 1, 0), axis=1, keepdims=True)
    slot = own_sub[:, 0:1] * TILE + rank
    pick = onehot(iota((2 * n, slots), 1) == jnp.concatenate([slot, slot + CAP], axis=0))
    load.wait()
    rows = dot(pick, got_ref[...].reshape(slots, HALF))
    low = base_ref[:, :HALF].astype(jnp.float32) + rows[:n]
    high = base_ref[:, HALF:].astype(jnp.float32) + rows[n:]
    square = jnp.sum(low * low, axis=1, keepdims=True) + jnp.sum(high * high, axis=1, keepdims=True)
    scale = lax.rsqrt(square * (1.0 / (2 * HALF)) + 1e-05)
    gain = gain_ref[0:1]
    normed_ref[:, :HALF] = (low * scale * gain[:, :HALF]).astype(jnp.bfloat16)
    normed_ref[:, HALF:] = (high * scale * gain[:, HALF:]).astype(jnp.bfloat16)
    for j, copy in enumerate(copies):
        copy.wait()
        if j + AHEAD < blocks:
            copies[j + AHEAD].start()
        part = normed_ref[:, j * depth : (j + 1) * depth]
        for first in range(0, columns, per):
            at = slice(first, first + per)
            made = dot(part, w_ref[j, :, at])
            if j > 0:
                made += total_ref[:, at]
            if j < blocks - 1:
                total_ref[:, at] = made
                continue
            made = made.astype(jnp.bfloat16)
            for i in range(per // HEAD):
                kind, head = divmod(first // HEAD + i, HEADS)
                made_ref[head, :, kind * HEAD : (kind + 1) * HEAD] = made[:, i * HEAD : (i + 1) * HEAD]
    me = lax.axis_index("ctx")
    for shift, ref in enumerate(out_refs):
        ref[...] = made_ref[(me + shift) % HEADS]


def spread_kernel(ids_ref, out_ref):
    out_ref[...] = jnp.broadcast_to(ids_ref[...][None], out_ref.shape)


def attention_kernel(block, *refs):
    *ins, mixed_ref, qkv_ref = refs
    tokens = ins[0].shape[0]
    seq = tokens * HEADS
    me = lax.axis_index("ctx")
    for shift, ref in enumerate(ins):
        source = (me + HEADS - shift) % HEADS
        qkv_ref[pl.ds(pl.multiple_of(source * tokens, tokens), tokens), :] = ref[...]
    lanes = (((1,), (1,)), ((), ()))
    allowed = iota((block, block), 1) <= iota((block, block), 0)
    for i in range(seq // block):
        here = slice(i * block, (i + 1) * block)
        query = qkv_ref[here, :HEAD]
        scores = dot(query, qkv_ref[here, HEAD : 2 * HEAD], lanes) * HEAD ** (-0.5)
        scores = jnp.where(allowed, scores, -1e30)
        top = jnp.max(scores, axis=1, keepdims=True)
        if i > 0:
            before = dot(query, qkv_ref[: i * block, HEAD : 2 * HEAD], lanes) * HEAD ** (-0.5)
            top = jnp.maximum(top, jnp.max(before, axis=1, keepdims=True))
        weights = jnp.where(allowed, jnp.exp(scores - top), 0.0)
        total = jnp.sum(weights, axis=1, keepdims=True)
        mixed = dot(weights.astype(jnp.bfloat16), qkv_ref[here, 2 * HEAD :])
        if i > 0:
            weights = jnp.exp(before - top)
            total += jnp.sum(weights, axis=1, keepdims=True)
            mixed += dot(weights.astype(jnp.bfloat16), qkv_ref[: i * block, 2 * HEAD :])
        mixed_ref[here, :] = (mixed / total).astype(jnp.bfloat16)


def call(kernel, out, flops, moved, mb=24, **kwargs):
    return pl.pallas_call(
        kernel,
        out_shape=out,
        compiler_params=pltpu.CompilerParams(vmem_limit_bytes=mb * MB),
        cost_estimate=pl.CostEstimate(flops=flops, bytes_accessed=moved, transcendentals=0),
        **kwargs,
    )


def exchange(x, axes):
    return lax.all_to_all(x, axes, split_axis=0, concat_axis=0, tiled=True)


def shift_all(pieces):
    n = len(pieces)
    moved = [
        lax.ppermute(pieces[k], "ctx", [(i, (i + k) % n) for i in range(n)]) for k in range(1, n)
    ]
    return [pieces[0], *moved]


def shards(base_embed, ngram_ids, ngram_table, embed_cot, norm_gain, w_qkv):
    tokens = ngram_ids.shape[1]
    width = base_embed.shape[2]
    held = ngram_table.shape[0]
    table = lax.axis_size("table")
    ctx = lax.axis_size("ctx")
    owners = table * ctx
    slots = owners * TILE
    columns = w_qkv.shape[1]
    bf16, f32 = jnp.bfloat16, jnp.float32
    shape = jax.ShapeDtypeStruct
    whole = pl.BlockSpec(memory_space=pltpu.VMEM)
    remote = pl.BlockSpec(memory_space=pltpu.HBM)

    near_hbm = pltpu.with_memory_space_constraint(ngram_ids, pltpu.HBM)
    all_ids = exchange(
        call(spread_kernel, shape((owners, 1, tokens), jnp.int32), 0, 0, name="spread")(near_hbm), BOTH
    )
    blocks = pltpu.HBM((owners, 2, TILE, HALF), bf16)
    stage = pltpu.VMEM((owners, TILE, HALF), bf16)
    send = call(
        functools.partial(pack_kernel, held),
        blocks,
        2 * slots * tokens * width,
        3 * MB,
        name="pack",
        in_specs=[whole] * 2,
        out_specs=remote,
        scratch_shapes=[stage, pltpu.SemaphoreType.DMA],
    )(ngram_ids, embed_cot[0])
    send = call(
        rows_kernel,
        blocks,
        2 * slots * held * width,
        4 * MB,
        name="rows",
        in_specs=[whole, whole, remote],
        out_specs=remote,
        scratch_shapes=[stage, pltpu.SemaphoreType.DMA((4,))],
        input_output_aliases={2: 0},
    )(all_ids, ngram_table, send)
    got = exchange(send, BOTH)
    low, high, gain = call(
        prepare_kernel,
        [pltpu.VMEM((held, slots), bf16)] * 2 + [shape((8, width), f32)],
        20000 * MB,
        2 * MB,
        name="prepare",
    )(all_ids, norm_gain.reshape(1, width))
    w_blocks = 8
    qkv = call(
        functools.partial(qkv_kernel, held),
        [shape((tokens, 3 * HEAD), bf16)] * HEADS,
        2 * tokens * width * columns,
        16 * MB,
        name="qkv",
        in_specs=[whole, remote, whole, whole, remote, remote, remote],
        out_specs=[whole] * HEADS,
        scratch_shapes=[
            stage,
            pltpu.VMEM((w_blocks, width // w_blocks, columns), bf16),
            pltpu.VMEM((tokens, width), bf16),
            pltpu.VMEM((tokens, columns), f32),
            pltpu.VMEM((HEADS, tokens, 3 * HEAD), bf16),
            pltpu.SemaphoreType.DMA((w_blocks + 1,)),
        ],
    )(
        ngram_ids,
        got,
        base_embed[0],
        gain,
        pltpu.with_memory_space_constraint(w_qkv, pltpu.HBM),
        low,
        high,
    )
    steps = 4
    per = width // steps
    table_grad = call(
        grad_kernel,
        shape((held, width), f32),
        2 * slots * held * width,
        6 * MB,
        name="grad",
        grid=(steps,),
        in_specs=[
            pl.BlockSpec((held, slots), lambda j: (0, 0)),
            pl.BlockSpec((held, slots), lambda j: (0, 0)),
            pl.BlockSpec((owners, None, TILE, per), lambda j: (0, 1, 0, j // 2)),
        ],
        out_specs=pl.BlockSpec((held, per), lambda j: (0, j % 2 * 2 + j // 2)),
    )(low, high, got)
    mixed = call(
        functools.partial(attention_kernel, 256),
        shape((ctx * tokens, HEAD), bf16),
        4 * ctx * tokens * ctx * tokens * HEAD,
        2 * MB,
        name="attention",
        scratch_shapes=[pltpu.VMEM((ctx * tokens, 3 * HEAD), bf16)],
    )(*shift_all(qkv))
    context = exchange(mixed.reshape(ctx, tokens, HEAD), "ctx")
    context = context.transpose(1, 0, 2).reshape(tokens, HEADS * HEAD)
    return (context[None], table_grad)


def solution(mesh):
    return jax.shard_map(
        shards,
        mesh=mesh,
        in_specs=(
            P("table", "ctx", None),
            P("table", "ctx"),
            P(("table", "ctx"), None),
            P("table", "ctx", None),
            P(),
            P(),
        ),
        out_specs=(P("table", "ctx", None), P(("table", "ctx"), None)),
        check_vma=False,
    )
```

```python
import functools

import jax
import jax.numpy as jnp
from jax import lax
from jax.experimental import pallas as pl
from jax.experimental.pallas import tpu as pltpu
from jax.sharding import PartitionSpec as P

HEAD = 128
HEADS = 8
CAP = 4
TILE = 2 * CAP
HALF = 1024
MB = 1024 * 1024
AHEAD = 4
BOTH = ("table", "ctx")


def iota(shape, dim):
    return lax.broadcasted_iota(jnp.int32, shape, dim)


def dot(a, b, dims=(((1,), (0,)), ((), ()))):
    return lax.dot_general(a, b, dims, preferred_element_type=jnp.float32)


def onehot(mask):
    return jnp.where(mask, 1.0, 0.0).astype(jnp.bfloat16)


def owner_grid(ids, held):
    n = ids.shape[1]
    owner = jnp.broadcast_to(ids, (n, n)) // held
    return owner, owner.astype(jnp.float32).T.astype(jnp.int32)


def asked_rows(ids_ref, held):
    n, _, tokens = ids_ref.shape
    me = lax.axis_index("table") * lax.axis_size("ctx") + lax.axis_index("ctx")
    wide = jnp.broadcast_to(ids_ref[...], (n, TILE, tokens)).reshape(n * TILE, tokens)
    local = wide - me * held
    mine = (local >= 0) & (local < held)
    earlier = onehot(iota((tokens, tokens), 0) < iota((tokens, tokens), 1))
    rank = dot(onehot(mine), earlier)
    slot = (iota(wide.shape, 0) % CAP).astype(jnp.float32)
    return jnp.where(mine & (rank == slot), local + 1, 0)


def pack_kernel(held, ids_ref, cot_ref, send_hbm, stage_ref, sem):
    tokens = ids_ref.shape[1]
    own_lane, own_sub = owner_grid(ids_ref[...], held)
    earlier = iota((tokens, tokens), 0) < iota((tokens, tokens), 1)
    rank = jnp.sum(jnp.where((own_lane == own_sub) & earlier, 1, 0), axis=0, keepdims=True)
    slot = own_lane[0:1] * TILE + rank
    at = iota((stage_ref.shape[0] * TILE, tokens), 0)
    made = dot(onehot(at == slot), cot_ref[:, :HALF]) + dot(onehot(at == slot + CAP), cot_ref[:, HALF:])
    stage_ref[...] = made.astype(jnp.bfloat16).reshape(stage_ref.shape)
    copy = pltpu.make_async_copy(stage_ref, send_hbm.at[:, 1], sem)
    copy.start()
    copy.wait()


def rows_kernel(ids_ref, table_ref, cot_hbm, send_hbm, stage_ref, sems):
    held = table_ref.shape[0]
    asked = asked_rows(ids_ref, held)
    row = jnp.sum(asked.astype(jnp.float32), axis=1, keepdims=True).astype(jnp.int32)
    parts = sems.shape[0]
    block = row.shape[0] // parts
    shape = (block, held)
    upper = iota(shape, 0) % TILE >= CAP
    copies = []
    for part in range(parts):
        hit = row[part * block : (part + 1) * block] == iota(shape, 1) + 1
        made = dot(onehot(hit & ~upper), table_ref[:, :HALF]) + dot(
            onehot(hit & upper), table_ref[:, HALF:]
        )
        at = pl.ds(part * (block // TILE), block // TILE)
        stage_ref[at] = made.astype(jnp.bfloat16).reshape(block // TILE, TILE, HALF)
        copies.append(
            pltpu.make_async_copy(stage_ref.at[at], send_hbm.at[at, 0], sems.at[part])
        )
        copies[-1].start()
    for copy in copies:
        copy.wait()


def prepare_kernel(ids_ref, gain_ref, low_ref, high_ref, wide_gain_ref):
    wide_gain_ref[...] = jnp.broadcast_to(gain_ref[...].astype(jnp.float32), wide_gain_ref.shape)
    asked = asked_rows(ids_ref, low_ref.shape[0])
    lanes = (((1,), (1,)), ((), ()))
    ones = jnp.ones((8, asked.shape[1]), jnp.bfloat16)
    top = asked // 256
    row = 256.0 * dot(ones, top.astype(jnp.float32).astype(jnp.bfloat16), lanes) + dot(
        ones, (asked - top * 256).astype(jnp.float32).astype(jnp.bfloat16), lanes
    )
    shape = low_ref.shape
    hit = row[0:1].astype(jnp.int32) == iota(shape, 0) + 1
    upper = iota(shape, 1) % TILE >= CAP
    low_ref[...] = onehot(hit & ~upper)
    high_ref[...] = onehot(hit & upper)


def grad_kernel(low_ref, high_ref, cot_ref, grad_ref):
    step = pl.program_id(0)
    cot = cot_ref[...].reshape(low_ref.shape[1], grad_ref.shape[1])

    @pl.when(step % 2 == 0)
    def _():
        grad_ref[...] = dot(low_ref[...], cot)

    @pl.when(step % 2 == 1)
    def _():
        grad_ref[...] = dot(high_ref[...], cot)


def qkv_kernel(
    held, ids_ref, got_hbm, base_ref, gain_ref, w_hbm, low_hbm, high_hbm, *refs
):
    *out_refs, got_ref, w_ref, normed_ref, total_ref, made_ref, sems = refs
    blocks, depth, columns = w_ref.shape
    per = columns // 6
    load = pltpu.make_async_copy(got_hbm.at[:, 0], got_ref, sems.at[blocks])
    load.start()
    copies = [
        pltpu.make_async_copy(w_hbm.at[j * depth : (j + 1) * depth], w_ref.at[j], sems.at[j])
        for j in range(blocks)
    ]
    for copy in copies[:AHEAD]:
        copy.start()
    n = ids_ref.shape[1]
    slots = got_ref.shape[0] * TILE
    own_lane, own_sub = owner_grid(ids_ref[...], held)
    same = (own_lane == own_sub) & (iota((n, n), 1) < iota((n, n), 0))
    rank = jnp.sum(jnp.where(same, 1, 0), axis=1, keepdims=True)
    slot = own_sub[:, 0:1] * TILE + rank
    pick = onehot(iota((2 * n, slots), 1) == jnp.concatenate([slot, slot + CAP], axis=0))
    load.wait()
    rows = dot(pick, got_ref[...].reshape(slots, HALF))
    low = base_ref[:, :HALF].astype(jnp.float32) + rows[:n]
    high = base_ref[:, HALF:].astype(jnp.float32) + rows[n:]
    square = jnp.sum(low * low, axis=1, keepdims=True) + jnp.sum(high * high, axis=1, keepdims=True)
    scale = lax.rsqrt(square * (1.0 / (2 * HALF)) + 1e-05)
    gain = gain_ref[0:1]
    normed_ref[:, :HALF] = (low * scale * gain[:, :HALF]).astype(jnp.bfloat16)
    normed_ref[:, HALF:] = (high * scale * gain[:, HALF:]).astype(jnp.bfloat16)
    for j, copy in enumerate(copies):
        copy.wait()
        if j + AHEAD < blocks:
            copies[j + AHEAD].start()
        part = normed_ref[:, j * depth : (j + 1) * depth]
        for first in range(0, columns, per):
            at = slice(first, first + per)
            made = dot(part, w_ref[j, :, at])
            if j > 0:
                made += total_ref[:, at]
            if j < blocks - 1:
                total_ref[:, at] = made
                continue
            made = made.astype(jnp.bfloat16)
            for i in range(per // HEAD):
                kind, head = divmod(first // HEAD + i, HEADS)
                made_ref[head, :, kind * HEAD : (kind + 1) * HEAD] = made[:, i * HEAD : (i + 1) * HEAD]
    me = lax.axis_index("ctx")
    for shift, ref in enumerate(out_refs):
        ref[...] = made_ref[(me + shift) % HEADS]


def spread_kernel(ids_ref, out_ref):
    out_ref[...] = jnp.broadcast_to(ids_ref[...][None], out_ref.shape)


def attention_kernel(block, *refs):
    *ins, mixed_hbm, qkv_ref, mixed_ref, sems = refs
    tokens = ins[0].shape[0]
    seq = tokens * HEADS
    me = lax.axis_index("ctx")
    for shift, ref in enumerate(ins):
        source = (me + HEADS - shift) % HEADS
        qkv_ref[pl.ds(pl.multiple_of(source * tokens, tokens), tokens), :] = ref[...]
    lanes = (((1,), (1,)), ((), ()))
    allowed = iota((block, block), 1) <= iota((block, block), 0)
    stores = []
    for i in range(seq // block):
        here = slice(i * block, (i + 1) * block)
        query = qkv_ref[here, :HEAD]
        scores = dot(query, qkv_ref[here, HEAD : 2 * HEAD], lanes) * HEAD ** (-0.5)
        scores = jnp.where(allowed, scores, -1e30)
        top = jnp.max(scores, axis=1, keepdims=True)
        if i > 0:
            before = dot(query, qkv_ref[: i * block, HEAD : 2 * HEAD], lanes) * HEAD ** (-0.5)
            top = jnp.maximum(top, jnp.max(before, axis=1, keepdims=True))
        weights = jnp.where(allowed, jnp.exp(scores - top), 0.0)
        total = jnp.sum(weights, axis=1, keepdims=True)
        mixed = dot(weights.astype(jnp.bfloat16), qkv_ref[here, 2 * HEAD :])
        if i > 0:
            weights = jnp.exp(before - top)
            total += jnp.sum(weights, axis=1, keepdims=True)
            mixed += dot(weights.astype(jnp.bfloat16), qkv_ref[: i * block, 2 * HEAD :])
        mixed_ref[here, :] = (mixed / total).astype(jnp.bfloat16)
        stores.append(
            pltpu.make_async_copy(mixed_ref.at[here], mixed_hbm.at[here], sems.at[i])
        )
        stores[-1].start()
    for store in stores:
        store.wait()


def join_kernel(heads_ref, out_ref):
    for h in range(HEADS):
        out_ref[:, h * HEAD : (h + 1) * HEAD] = heads_ref[h]


def call(kernel, out, flops, moved, mb=24, **kwargs):
    return pl.pallas_call(
        kernel,
        out_shape=out,
        compiler_params=pltpu.CompilerParams(vmem_limit_bytes=mb * MB),
        cost_estimate=pl.CostEstimate(flops=flops, bytes_accessed=moved, transcendentals=0),
        **kwargs,
    )


def exchange(x, axes):
    return lax.all_to_all(x, axes, split_axis=0, concat_axis=0, tiled=True)


def shift_all(pieces):
    n = len(pieces)
    moved = [
        lax.ppermute(pieces[k], "ctx", [(i, (i + k) % n) for i in range(n)]) for k in range(1, n)
    ]
    return [pieces[0], *moved]


def shards(base_embed, ngram_ids, ngram_table, embed_cot, norm_gain, w_qkv):
    tokens = ngram_ids.shape[1]
    width = base_embed.shape[2]
    held = ngram_table.shape[0]
    table = lax.axis_size("table")
    ctx = lax.axis_size("ctx")
    owners = table * ctx
    slots = owners * TILE
    columns = w_qkv.shape[1]
    bf16, f32 = jnp.bfloat16, jnp.float32
    shape = jax.ShapeDtypeStruct
    whole = pl.BlockSpec(memory_space=pltpu.VMEM)
    remote = pl.BlockSpec(memory_space=pltpu.HBM)

    all_ids = exchange(
        call(spread_kernel, pltpu.VMEM((owners, 1, tokens), jnp.int32), 0, 0, name="spread")(
            ngram_ids
        ),
        BOTH,
    )
    blocks = pltpu.HBM((owners, 2, TILE, HALF), bf16)
    stage = pltpu.VMEM((owners, TILE, HALF), bf16)
    send = call(
        functools.partial(pack_kernel, held),
        blocks,
        2 * slots * tokens * width,
        3 * MB,
        name="pack",
        in_specs=[whole] * 2,
        out_specs=remote,
        scratch_shapes=[stage, pltpu.SemaphoreType.DMA],
    )(ngram_ids, embed_cot[0])
    send = call(
        rows_kernel,
        blocks,
        2 * slots * held * width,
        4 * MB,
        name="rows",
        in_specs=[whole, whole, remote],
        out_specs=remote,
        scratch_shapes=[stage, pltpu.SemaphoreType.DMA((4,))],
        input_output_aliases={2: 0},
    )(all_ids, ngram_table, send)
    got = exchange(send, BOTH)
    low, high, gain = call(
        prepare_kernel,
        [pltpu.VMEM((held, slots), bf16)] * 2 + [shape((8, width), f32)],
        20000 * MB,
        2 * MB,
        name="prepare",
    )(all_ids, norm_gain.reshape(1, width))
    w_blocks = 8
    qkv = call(
        functools.partial(qkv_kernel, held),
        [shape((tokens, 3 * HEAD), bf16)] * HEADS,
        2 * tokens * width * columns,
        16 * MB,
        name="qkv",
        in_specs=[whole, remote, whole, whole, remote, remote, remote],
        out_specs=[whole] * HEADS,
        scratch_shapes=[
            stage,
            pltpu.VMEM((w_blocks, width // w_blocks, columns), bf16),
            pltpu.VMEM((tokens, width), bf16),
            pltpu.VMEM((tokens, columns), f32),
            pltpu.VMEM((HEADS, tokens, 3 * HEAD), bf16),
            pltpu.SemaphoreType.DMA((w_blocks + 1,)),
        ],
    )(
        ngram_ids,
        got,
        base_embed[0],
        gain,
        pltpu.with_memory_space_constraint(w_qkv, pltpu.HBM),
        low,
        high,
    )
    steps = 4
    per = width // steps
    table_grad = call(
        grad_kernel,
        shape((held, width), f32),
        2 * slots * held * width,
        6 * MB,
        name="grad",
        grid=(steps,),
        in_specs=[
            pl.BlockSpec((held, slots), lambda j: (0, 0)),
            pl.BlockSpec((held, slots), lambda j: (0, 0)),
            pl.BlockSpec((owners, None, TILE, per), lambda j: (0, 1, 0, j // 2)),
        ],
        out_specs=pl.BlockSpec((held, per), lambda j: (0, j % 2 * 2 + j // 2)),
    )(low, high, got)
    mixed = call(
        functools.partial(attention_kernel, 256),
        pltpu.HBM((ctx * tokens, HEAD), bf16),
        4 * ctx * tokens * ctx * tokens * HEAD,
        2 * MB,
        name="attention",
        in_specs=[whole] * HEADS,
        out_specs=remote,
        scratch_shapes=[
            pltpu.VMEM((ctx * tokens, 3 * HEAD), bf16),
            pltpu.VMEM((ctx * tokens, HEAD), bf16),
            pltpu.SemaphoreType.DMA((ctx * tokens // 256,)),
        ],
    )(*shift_all(qkv))
    context = exchange(mixed.reshape(ctx, tokens, HEAD), "ctx")
    context = call(
        join_kernel, shape((tokens, HEADS * HEAD), bf16), 0, MB // 2, name="join"
    )(context)
    return (context[None], table_grad)


def solution(mesh):
    return jax.shard_map(
        shards,
        mesh=mesh,
        in_specs=(
            P("table", "ctx", None),
            P("table", "ctx"),
            P(("table", "ctx"), None),
            P("table", "ctx", None),
            P(),
            P(),
        ),
        out_specs=(P("table", "ctx", None), P(("table", "ctx"), None)),
        check_vma=False,
    )
```

```python
import functools

import jax
import jax.numpy as jnp
from jax import lax
from jax.experimental import pallas as pl
from jax.experimental.pallas import tpu as pltpu
from jax.sharding import PartitionSpec as P

HEAD = 128
HEADS = 8
CAP = 4
TILE = 2 * CAP
HALF = 1024
MB = 1024 * 1024
AHEAD = 4
BOTH = ("ctx", "table")


def iota(shape, dim):
    return lax.broadcasted_iota(jnp.int32, shape, dim)


def dot(a, b, dims=(((1,), (0,)), ((), ()))):
    return lax.dot_general(a, b, dims, preferred_element_type=jnp.float32)


def onehot(mask):
    return jnp.where(mask, 1.0, 0.0).astype(jnp.bfloat16)


def owner_grid(ids, held):
    n = ids.shape[1]
    owner = jnp.broadcast_to(ids, (n, n)) // held
    return owner, owner.astype(jnp.float32).T.astype(jnp.int32)


def position(owner):
    ctx = lax.axis_size("ctx")
    return owner % ctx * lax.axis_size("table") + owner // ctx


def asked_rows(ids_ref, held):
    n, _, tokens = ids_ref.shape
    me = lax.axis_index("table") * lax.axis_size("ctx") + lax.axis_index("ctx")
    wide = jnp.broadcast_to(ids_ref[...], (n, TILE, tokens)).reshape(n * TILE, tokens)
    local = wide - me * held
    mine = (local >= 0) & (local < held)
    earlier = onehot(iota((tokens, tokens), 0) < iota((tokens, tokens), 1))
    rank = dot(onehot(mine), earlier)
    slot = (iota(wide.shape, 0) % CAP).astype(jnp.float32)
    return jnp.where(mine & (rank == slot), local + 1, 0)


def pack_kernel(held, ids_ref, cot_ref, send_hbm, stage_ref, sem):
    tokens = ids_ref.shape[1]
    own_lane, own_sub = owner_grid(ids_ref[...], held)
    earlier = iota((tokens, tokens), 0) < iota((tokens, tokens), 1)
    rank = jnp.sum(jnp.where((own_lane == own_sub) & earlier, 1, 0), axis=0, keepdims=True)
    slot = position(own_lane[0:1]) * TILE + rank
    at = iota((stage_ref.shape[0] * TILE, tokens), 0)
    made = dot(onehot(at == slot), cot_ref[:, :HALF]) + dot(onehot(at == slot + CAP), cot_ref[:, HALF:])
    stage_ref[...] = made.astype(jnp.bfloat16).reshape(stage_ref.shape)
    copy = pltpu.make_async_copy(stage_ref, send_hbm.at[:, 1], sem)
    copy.start()
    copy.wait()


def rows_kernel(ids_ref, table_ref, cot_hbm, send_hbm, stage_ref, sems):
    held = table_ref.shape[0]
    asked = asked_rows(ids_ref, held)
    row = jnp.sum(asked.astype(jnp.float32), axis=1, keepdims=True).astype(jnp.int32)
    parts = sems.shape[0]
    block = row.shape[0] // parts
    shape = (block, held)
    upper = iota(shape, 0) % TILE >= CAP
    copies = []
    for part in range(parts):
        hit = row[part * block : (part + 1) * block] == iota(shape, 1) + 1
        made = dot(onehot(hit & ~upper), table_ref[:, :HALF]) + dot(
            onehot(hit & upper), table_ref[:, HALF:]
        )
        at = pl.ds(part * (block // TILE), block // TILE)
        stage_ref[at] = made.astype(jnp.bfloat16).reshape(block // TILE, TILE, HALF)
        copies.append(
            pltpu.make_async_copy(stage_ref.at[at], send_hbm.at[at, 0], sems.at[part])
        )
        copies[-1].start()
    for copy in copies:
        copy.wait()


def prepare_kernel(ids_ref, gain_ref, low_ref, high_ref, wide_gain_ref):
    wide_gain_ref[...] = jnp.broadcast_to(gain_ref[...].astype(jnp.float32), wide_gain_ref.shape)
    asked = asked_rows(ids_ref, low_ref.shape[0])
    lanes = (((1,), (1,)), ((), ()))
    ones = jnp.ones((8, asked.shape[1]), jnp.bfloat16)
    top = asked // 256
    row = 256.0 * dot(ones, top.astype(jnp.float32).astype(jnp.bfloat16), lanes) + dot(
        ones, (asked - top * 256).astype(jnp.float32).astype(jnp.bfloat16), lanes
    )
    shape = low_ref.shape
    hit = row[0:1].astype(jnp.int32) == iota(shape, 0) + 1
    upper = iota(shape, 1) % TILE >= CAP
    low_ref[...] = onehot(hit & ~upper)
    high_ref[...] = onehot(hit & upper)


def grad_kernel(low_ref, high_ref, cot_ref, grad_ref):
    step = pl.program_id(0)
    cot = cot_ref[...].reshape(low_ref.shape[1], grad_ref.shape[1])

    @pl.when(step % 2 == 0)
    def _():
        grad_ref[...] = dot(low_ref[...], cot)

    @pl.when(step % 2 == 1)
    def _():
        grad_ref[...] = dot(high_ref[...], cot)


def qkv_kernel(
    held, ids_ref, got_hbm, base_ref, gain_ref, w_hbm, low_hbm, high_hbm, *refs
):
    *out_refs, got_ref, w_ref, normed_ref, total_ref, made_ref, sems = refs
    blocks, depth, columns = w_ref.shape
    per = columns // 6
    load = pltpu.make_async_copy(got_hbm.at[:, 0], got_ref, sems.at[blocks])
    load.start()
    copies = [
        pltpu.make_async_copy(w_hbm.at[j * depth : (j + 1) * depth], w_ref.at[j], sems.at[j])
        for j in range(blocks)
    ]
    for copy in copies[:AHEAD]:
        copy.start()
    n = ids_ref.shape[1]
    slots = got_ref.shape[0] * TILE
    own_lane, own_sub = owner_grid(ids_ref[...], held)
    same = (own_lane == own_sub) & (iota((n, n), 1) < iota((n, n), 0))
    rank = jnp.sum(jnp.where(same, 1, 0), axis=1, keepdims=True)
    slot = position(own_sub[:, 0:1]) * TILE + rank
    pick = onehot(iota((2 * n, slots), 1) == jnp.concatenate([slot, slot + CAP], axis=0))
    load.wait()
    rows = dot(pick, got_ref[...].reshape(slots, HALF))
    low = base_ref[:, :HALF].astype(jnp.float32) + rows[:n]
    high = base_ref[:, HALF:].astype(jnp.float32) + rows[n:]
    square = jnp.sum(low * low, axis=1, keepdims=True) + jnp.sum(high * high, axis=1, keepdims=True)
    scale = lax.rsqrt(square * (1.0 / (2 * HALF)) + 1e-05)
    gain = gain_ref[0:1]
    normed_ref[:, :HALF] = (low * scale * gain[:, :HALF]).astype(jnp.bfloat16)
    normed_ref[:, HALF:] = (high * scale * gain[:, HALF:]).astype(jnp.bfloat16)
    for j, copy in enumerate(copies):
        copy.wait()
        if j + AHEAD < blocks:
            copies[j + AHEAD].start()
        part = normed_ref[:, j * depth : (j + 1) * depth]
        for first in range(0, columns, per):
            at = slice(first, first + per)
            made = dot(part, w_ref[j, :, at])
            if j > 0:
                made += total_ref[:, at]
            if j < blocks - 1:
                total_ref[:, at] = made
                continue
            made = made.astype(jnp.bfloat16)
            for i in range(per // HEAD):
                kind, head = divmod(first // HEAD + i, HEADS)
                made_ref[head, :, kind * HEAD : (kind + 1) * HEAD] = made[:, i * HEAD : (i + 1) * HEAD]
    me = lax.axis_index("ctx")
    for shift, ref in enumerate(out_refs):
        ref[...] = made_ref[(me + shift) % HEADS]


def spread_kernel(ids_ref, out_ref):
    out_ref[...] = jnp.broadcast_to(ids_ref[...][None], out_ref.shape)


def attention_kernel(block, *refs):
    *ins, mixed_hbm, qkv_ref, mixed_ref, sems = refs
    tokens = ins[0].shape[0]
    seq = tokens * HEADS
    me = lax.axis_index("ctx")
    for shift, ref in enumerate(ins):
        source = (me + HEADS - shift) % HEADS
        qkv_ref[pl.ds(pl.multiple_of(source * tokens, tokens), tokens), :] = ref[...]
    lanes = (((1,), (1,)), ((), ()))
    allowed = iota((block, block), 1) <= iota((block, block), 0)
    stores = []
    for i in range(seq // block):
        here = slice(i * block, (i + 1) * block)
        query = qkv_ref[here, :HEAD]
        scores = dot(query, qkv_ref[here, HEAD : 2 * HEAD], lanes) * HEAD ** (-0.5)
        scores = jnp.where(allowed, scores, -1e30)
        top = jnp.max(scores, axis=1, keepdims=True)
        if i > 0:
            before = dot(query, qkv_ref[: i * block, HEAD : 2 * HEAD], lanes) * HEAD ** (-0.5)
            top = jnp.maximum(top, jnp.max(before, axis=1, keepdims=True))
        weights = jnp.where(allowed, jnp.exp(scores - top), 0.0)
        total = jnp.sum(weights, axis=1, keepdims=True)
        mixed = dot(weights.astype(jnp.bfloat16), qkv_ref[here, 2 * HEAD :])
        if i > 0:
            weights = jnp.exp(before - top)
            total += jnp.sum(weights, axis=1, keepdims=True)
            mixed += dot(weights.astype(jnp.bfloat16), qkv_ref[: i * block, 2 * HEAD :])
        mixed_ref[here, :] = (mixed / total).astype(jnp.bfloat16)
        stores.append(
            pltpu.make_async_copy(mixed_ref.at[here], mixed_hbm.at[here], sems.at[i])
        )
        stores[-1].start()
    for store in stores:
        store.wait()


def join_kernel(heads_ref, out_ref):
    for h in range(HEADS):
        out_ref[:, h * HEAD : (h + 1) * HEAD] = heads_ref[h]


def call(kernel, out, flops, moved, mb=24, **kwargs):
    return pl.pallas_call(
        kernel,
        out_shape=out,
        compiler_params=pltpu.CompilerParams(vmem_limit_bytes=mb * MB),
        cost_estimate=pl.CostEstimate(flops=flops, bytes_accessed=moved, transcendentals=0),
        **kwargs,
    )


def exchange(x, axes):
    return lax.all_to_all(x, axes, split_axis=0, concat_axis=0, tiled=True)


def shift_all(pieces):
    n = len(pieces)
    moved = [
        lax.ppermute(pieces[k], "ctx", [(i, (i + k) % n) for i in range(n)]) for k in range(1, n)
    ]
    return [pieces[0], *moved]


def shards(base_embed, ngram_ids, ngram_table, embed_cot, norm_gain, w_qkv):
    tokens = ngram_ids.shape[1]
    width = base_embed.shape[2]
    held = ngram_table.shape[0]
    table = lax.axis_size("table")
    ctx = lax.axis_size("ctx")
    owners = table * ctx
    slots = owners * TILE
    columns = w_qkv.shape[1]
    bf16, f32 = jnp.bfloat16, jnp.float32
    shape = jax.ShapeDtypeStruct
    whole = pl.BlockSpec(memory_space=pltpu.VMEM)
    remote = pl.BlockSpec(memory_space=pltpu.HBM)

    all_ids = exchange(
        call(spread_kernel, pltpu.VMEM((owners, 1, tokens), jnp.int32), 0, 0, name="spread")(
            ngram_ids
        ),
        BOTH,
    )
    blocks = pltpu.HBM((owners, 2, TILE, HALF), bf16)
    stage = pltpu.VMEM((owners, TILE, HALF), bf16)
    send = call(
        functools.partial(pack_kernel, held),
        blocks,
        2 * slots * tokens * width,
        3 * MB,
        name="pack",
        in_specs=[whole] * 2,
        out_specs=remote,
        scratch_shapes=[stage, pltpu.SemaphoreType.DMA],
    )(ngram_ids, embed_cot[0])
    send = call(
        rows_kernel,
        blocks,
        2 * slots * held * width,
        4 * MB,
        name="rows",
        in_specs=[whole, whole, remote],
        out_specs=remote,
        scratch_shapes=[stage, pltpu.SemaphoreType.DMA((4,))],
        input_output_aliases={2: 0},
    )(all_ids, ngram_table, send)
    got = exchange(send, BOTH)
    low, high, gain = call(
        prepare_kernel,
        [pltpu.VMEM((held, slots), bf16)] * 2 + [shape((8, width), f32)],
        20000 * MB,
        2 * MB,
        name="prepare",
    )(all_ids, norm_gain.reshape(1, width))
    w_blocks = 8
    qkv = call(
        functools.partial(qkv_kernel, held),
        [shape((tokens, 3 * HEAD), bf16)] * HEADS,
        2 * tokens * width * columns,
        16 * MB,
        name="qkv",
        in_specs=[whole, remote, whole, whole, remote, remote, remote],
        out_specs=[whole] * HEADS,
        scratch_shapes=[
            stage,
            pltpu.VMEM((w_blocks, width // w_blocks, columns), bf16),
            pltpu.VMEM((tokens, width), bf16),
            pltpu.VMEM((tokens, columns), f32),
            pltpu.VMEM((HEADS, tokens, 3 * HEAD), bf16),
            pltpu.SemaphoreType.DMA((w_blocks + 1,)),
        ],
    )(
        ngram_ids,
        got,
        base_embed[0],
        gain,
        pltpu.with_memory_space_constraint(w_qkv, pltpu.HBM),
        low,
        high,
    )
    steps = 4
    per = width // steps
    table_grad = call(
        grad_kernel,
        shape((held, width), f32),
        2 * slots * held * width,
        6 * MB,
        name="grad",
        grid=(steps,),
        in_specs=[
            pl.BlockSpec((held, slots), lambda j: (0, 0)),
            pl.BlockSpec((held, slots), lambda j: (0, 0)),
            pl.BlockSpec((owners, None, TILE, per), lambda j: (0, 1, 0, j // 2)),
        ],
        out_specs=pl.BlockSpec((held, per), lambda j: (0, j % 2 * 2 + j // 2)),
    )(low, high, got)
    mixed = call(
        functools.partial(attention_kernel, 256),
        pltpu.HBM((ctx * tokens, HEAD), bf16),
        4 * ctx * tokens * ctx * tokens * HEAD,
        2 * MB,
        name="attention",
        in_specs=[whole] * HEADS,
        out_specs=remote,
        scratch_shapes=[
            pltpu.VMEM((ctx * tokens, 3 * HEAD), bf16),
            pltpu.VMEM((ctx * tokens, HEAD), bf16),
            pltpu.SemaphoreType.DMA((ctx * tokens // 256,)),
        ],
    )(*shift_all(qkv))
    context = exchange(mixed.reshape(ctx, tokens, HEAD), "ctx")
    context = call(
        join_kernel, shape((tokens, HEADS * HEAD), bf16), 0, MB // 2, name="join"
    )(context)
    return (context[None], table_grad)


def solution(mesh):
    return jax.shard_map(
        shards,
        mesh=mesh,
        in_specs=(
            P("table", "ctx", None),
            P("table", "ctx"),
            P(("table", "ctx"), None),
            P("table", "ctx", None),
            P(),
            P(),
        ),
        out_specs=(P("table", "ctx", None), P(("table", "ctx"), None)),
        check_vma=False,
    )
```

```python
import functools

import jax
import jax.numpy as jnp
from jax import lax
from jax.experimental import pallas as pl
from jax.experimental.pallas import tpu as pltpu
from jax.sharding import PartitionSpec as P

HEAD = 128
HEADS = 8
CAP = 4
TILE = 2 * CAP
HALF = 1024
MB = 1024 * 1024
AHEAD = 3
BOTH = ("ctx", "table")


def iota(shape, dim):
    return lax.broadcasted_iota(jnp.int32, shape, dim)


def dot(a, b, dims=(((1,), (0,)), ((), ()))):
    return lax.dot_general(a, b, dims, preferred_element_type=jnp.float32)


def onehot(mask):
    return jnp.where(mask, 1.0, 0.0).astype(jnp.bfloat16)


def owner_grid(ids, held):
    n = ids.shape[1]
    owner = jnp.broadcast_to(ids, (n, n)) // held
    return owner, owner.astype(jnp.float32).T.astype(jnp.int32)


def position(owner):
    ctx = lax.axis_size("ctx")
    return owner % ctx * lax.axis_size("table") + owner // ctx


def asked_rows(ids_ref, held):
    n, _, tokens = ids_ref.shape
    me = lax.axis_index("table") * lax.axis_size("ctx") + lax.axis_index("ctx")
    wide = jnp.broadcast_to(ids_ref[...], (n, TILE, tokens)).reshape(n * TILE, tokens)
    local = wide - me * held
    mine = (local >= 0) & (local < held)
    earlier = onehot(iota((tokens, tokens), 0) < iota((tokens, tokens), 1))
    rank = dot(onehot(mine), earlier)
    slot = (iota(wide.shape, 0) % CAP).astype(jnp.float32)
    return jnp.where(mine & (rank == slot), local + 1, 0)


def pack_kernel(held, ids_ref, cot_ref, send_hbm, stage_ref, sem):
    tokens = ids_ref.shape[1]
    own_lane, own_sub = owner_grid(ids_ref[...], held)
    earlier = iota((tokens, tokens), 0) < iota((tokens, tokens), 1)
    rank = jnp.sum(jnp.where((own_lane == own_sub) & earlier, 1, 0), axis=0, keepdims=True)
    slot = position(own_lane[0:1]) * TILE + rank
    at = iota((stage_ref.shape[0] * TILE, tokens), 0)
    made = dot(onehot(at == slot), cot_ref[:, :HALF]) + dot(onehot(at == slot + CAP), cot_ref[:, HALF:])
    stage_ref[...] = made.astype(jnp.bfloat16).reshape(stage_ref.shape)
    copy = pltpu.make_async_copy(stage_ref, send_hbm.at[:, 1], sem)
    copy.start()
    copy.wait()


def rows_kernel(ids_ref, table_ref, cot_hbm, send_hbm, stage_ref, sems):
    held = table_ref.shape[0]
    asked = asked_rows(ids_ref, held)
    row = jnp.sum(asked.astype(jnp.float32), axis=1, keepdims=True).astype(jnp.int32)
    parts = sems.shape[0]
    block = row.shape[0] // parts
    shape = (block, held)
    upper = iota(shape, 0) % TILE >= CAP
    copies = []
    for part in range(parts):
        hit = row[part * block : (part + 1) * block] == iota(shape, 1) + 1
        made = dot(onehot(hit & ~upper), table_ref[:, :HALF]) + dot(
            onehot(hit & upper), table_ref[:, HALF:]
        )
        at = pl.ds(part * (block // TILE), block // TILE)
        stage_ref[at] = made.astype(jnp.bfloat16).reshape(block // TILE, TILE, HALF)
        copies.append(
            pltpu.make_async_copy(stage_ref.at[at], send_hbm.at[at, 0], sems.at[part])
        )
        copies[-1].start()
    for copy in copies:
        copy.wait()


def prepare_kernel(ids_ref, gain_ref, low_ref, high_ref, wide_gain_ref):
    wide_gain_ref[...] = jnp.broadcast_to(gain_ref[...].astype(jnp.float32), wide_gain_ref.shape)
    asked = asked_rows(ids_ref, low_ref.shape[0])
    lanes = (((1,), (1,)), ((), ()))
    ones = jnp.ones((8, asked.shape[1]), jnp.bfloat16)
    top = asked // 256
    row = 256.0 * dot(ones, top.astype(jnp.float32).astype(jnp.bfloat16), lanes) + dot(
        ones, (asked - top * 256).astype(jnp.float32).astype(jnp.bfloat16), lanes
    )
    shape = low_ref.shape
    hit = row[0:1].astype(jnp.int32) == iota(shape, 0) + 1
    upper = iota(shape, 1) % TILE >= CAP
    low_ref[...] = onehot(hit & ~upper)
    high_ref[...] = onehot(hit & upper)


def grad_kernel(low_ref, high_ref, cot_ref, grad_ref):
    step = pl.program_id(0)
    cot = cot_ref[...].reshape(low_ref.shape[1], grad_ref.shape[1])

    @pl.when(step % 2 == 0)
    def _():
        grad_ref[...] = dot(low_ref[...], cot)

    @pl.when(step % 2 == 1)
    def _():
        grad_ref[...] = dot(high_ref[...], cot)


def qkv_kernel(
    held, ids_ref, got_hbm, base_ref, gain_ref, w_hbm, low_hbm, high_hbm, *refs
):
    *out_refs, got_ref, w_ref, normed_ref, total_ref, made_ref, sems = refs
    blocks, depth, columns = w_ref.shape
    per = columns // 6
    load = pltpu.make_async_copy(got_hbm.at[:, 0], got_ref, sems.at[blocks])
    load.start()
    copies = [
        pltpu.make_async_copy(w_hbm.at[j * depth : (j + 1) * depth], w_ref.at[j], sems.at[j])
        for j in range(blocks)
    ]
    for copy in copies[:AHEAD]:
        copy.start()
    n = ids_ref.shape[1]
    slots = got_ref.shape[0] * TILE
    own_lane, own_sub = owner_grid(ids_ref[...], held)
    same = (own_lane == own_sub) & (iota((n, n), 1) < iota((n, n), 0))
    rank = jnp.sum(jnp.where(same, 1, 0), axis=1, keepdims=True)
    slot = position(own_sub[:, 0:1]) * TILE + rank
    pick = onehot(iota((2 * n, slots), 1) == jnp.concatenate([slot, slot + CAP], axis=0))
    load.wait()
    rows = dot(pick, got_ref[...].reshape(slots, HALF))
    low = base_ref[:, :HALF].astype(jnp.float32) + rows[:n]
    high = base_ref[:, HALF:].astype(jnp.float32) + rows[n:]
    square = jnp.sum(low * low, axis=1, keepdims=True) + jnp.sum(high * high, axis=1, keepdims=True)
    scale = lax.rsqrt(square * (1.0 / (2 * HALF)) + 1e-05)
    gain = gain_ref[0:1]
    normed_ref[:, :HALF] = (low * scale * gain[:, :HALF]).astype(jnp.bfloat16)
    normed_ref[:, HALF:] = (high * scale * gain[:, HALF:]).astype(jnp.bfloat16)
    for j, copy in enumerate(copies):
        copy.wait()
        if j + AHEAD < blocks:
            copies[j + AHEAD].start()
        part = normed_ref[:, j * depth : (j + 1) * depth]
        for first in range(0, columns, per):
            at = slice(first, first + per)
            made = dot(part, w_ref[j, :, at])
            if j > 0:
                made += total_ref[:, at]
            if j < blocks - 1:
                total_ref[:, at] = made
                continue
            made = made.astype(jnp.bfloat16)
            for i in range(per // HEAD):
                kind, head = divmod(first // HEAD + i, HEADS)
                made_ref[head, :, kind * HEAD : (kind + 1) * HEAD] = made[:, i * HEAD : (i + 1) * HEAD]
    me = lax.axis_index("ctx")
    for shift, ref in enumerate(out_refs):
        ref[...] = made_ref[(me + shift) % HEADS]


def spread_kernel(ids_ref, out_ref):
    out_ref[...] = jnp.broadcast_to(ids_ref[...][None], out_ref.shape)


def attention_kernel(block, *refs):
    *ins, mixed_hbm, qkv_ref, mixed_ref, sems = refs
    tokens = ins[0].shape[0]
    seq = tokens * HEADS
    me = lax.axis_index("ctx")
    for shift, ref in enumerate(ins):
        source = (me + HEADS - shift) % HEADS
        qkv_ref[pl.ds(pl.multiple_of(source * tokens, tokens), tokens), :] = ref[...]
    lanes = (((1,), (1,)), ((), ()))
    allowed = iota((block, block), 1) <= iota((block, block), 0)
    stores = []
    for i in range(seq // block):
        here = slice(i * block, (i + 1) * block)
        query = qkv_ref[here, :HEAD]
        scores = dot(query, qkv_ref[here, HEAD : 2 * HEAD], lanes) * HEAD ** (-0.5)
        scores = jnp.where(allowed, scores, -1e30)
        top = jnp.max(scores, axis=1, keepdims=True)
        if i > 0:
            before = dot(query, qkv_ref[: i * block, HEAD : 2 * HEAD], lanes) * HEAD ** (-0.5)
            top = jnp.maximum(top, jnp.max(before, axis=1, keepdims=True))
        weights = jnp.where(allowed, jnp.exp(scores - top), 0.0)
        total = jnp.sum(weights, axis=1, keepdims=True)
        mixed = dot(weights.astype(jnp.bfloat16), qkv_ref[here, 2 * HEAD :])
        if i > 0:
            weights = jnp.exp(before - top)
            total += jnp.sum(weights, axis=1, keepdims=True)
            mixed += dot(weights.astype(jnp.bfloat16), qkv_ref[: i * block, 2 * HEAD :])
        mixed_ref[here, :] = (mixed / total).astype(jnp.bfloat16)
        stores.append(
            pltpu.make_async_copy(mixed_ref.at[here], mixed_hbm.at[here], sems.at[i])
        )
        stores[-1].start()
    for store in stores:
        store.wait()


def join_kernel(heads_ref, out_ref):
    for h in range(HEADS):
        out_ref[:, h * HEAD : (h + 1) * HEAD] = heads_ref[h]


def call(kernel, out, flops, moved, mb=24, **kwargs):
    return pl.pallas_call(
        kernel,
        out_shape=out,
        compiler_params=pltpu.CompilerParams(vmem_limit_bytes=mb * MB),
        cost_estimate=pl.CostEstimate(flops=flops, bytes_accessed=moved, transcendentals=0),
        **kwargs,
    )


def exchange(x, axes):
    return lax.all_to_all(x, axes, split_axis=0, concat_axis=0, tiled=True)


def shift_all(pieces):
    n = len(pieces)
    moved = [
        lax.ppermute(pieces[k], "ctx", [(i, (i + k) % n) for i in range(n)]) for k in range(1, n)
    ]
    return [pieces[0], *moved]


def shards(base_embed, ngram_ids, ngram_table, embed_cot, norm_gain, w_qkv):
    tokens = ngram_ids.shape[1]
    width = base_embed.shape[2]
    held = ngram_table.shape[0]
    table = lax.axis_size("table")
    ctx = lax.axis_size("ctx")
    owners = table * ctx
    slots = owners * TILE
    columns = w_qkv.shape[1]
    bf16, f32 = jnp.bfloat16, jnp.float32
    shape = jax.ShapeDtypeStruct
    whole = pl.BlockSpec(memory_space=pltpu.VMEM)
    remote = pl.BlockSpec(memory_space=pltpu.HBM)

    all_ids = exchange(
        call(spread_kernel, pltpu.VMEM((owners, 1, tokens), jnp.int32), 0, 0, name="spread")(
            ngram_ids
        ),
        BOTH,
    )
    blocks = pltpu.HBM((owners, 2, TILE, HALF), bf16)
    stage = pltpu.VMEM((owners, TILE, HALF), bf16)
    send = call(
        functools.partial(pack_kernel, held),
        blocks,
        2 * slots * tokens * width,
        3 * MB,
        name="pack",
        in_specs=[whole] * 2,
        out_specs=remote,
        scratch_shapes=[stage, pltpu.SemaphoreType.DMA],
    )(ngram_ids, embed_cot[0])
    send = call(
        rows_kernel,
        blocks,
        2 * slots * held * width,
        4 * MB,
        name="rows",
        in_specs=[whole, whole, remote],
        out_specs=remote,
        scratch_shapes=[stage, pltpu.SemaphoreType.DMA((4,))],
        input_output_aliases={2: 0},
    )(all_ids, ngram_table, send)
    got = exchange(send, BOTH)
    low, high, gain = call(
        prepare_kernel,
        [pltpu.VMEM((held, slots), bf16)] * 2 + [shape((8, width), f32)],
        20000 * MB,
        2 * MB,
        name="prepare",
    )(all_ids, norm_gain.reshape(1, width))
    w_blocks = 4
    qkv = call(
        functools.partial(qkv_kernel, held),
        [shape((tokens, 3 * HEAD), bf16)] * HEADS,
        2 * tokens * width * columns,
        16 * MB,
        name="qkv",
        in_specs=[whole, remote, whole, whole, remote, remote, remote],
        out_specs=[whole] * HEADS,
        scratch_shapes=[
            stage,
            pltpu.VMEM((w_blocks, width // w_blocks, columns), bf16),
            pltpu.VMEM((tokens, width), bf16),
            pltpu.VMEM((tokens, columns), f32),
            pltpu.VMEM((HEADS, tokens, 3 * HEAD), bf16),
            pltpu.SemaphoreType.DMA((w_blocks + 1,)),
        ],
    )(
        ngram_ids,
        got,
        base_embed[0],
        gain,
        pltpu.with_memory_space_constraint(w_qkv, pltpu.HBM),
        low,
        high,
    )
    steps = 4
    per = width // steps
    table_grad = call(
        grad_kernel,
        shape((held, width), f32),
        2 * slots * held * width,
        6 * MB,
        name="grad",
        grid=(steps,),
        in_specs=[
            pl.BlockSpec((held, slots), lambda j: (0, 0)),
            pl.BlockSpec((held, slots), lambda j: (0, 0)),
            pl.BlockSpec((owners, None, TILE, per), lambda j: (0, 1, 0, j // 2)),
        ],
        out_specs=pl.BlockSpec((held, per), lambda j: (0, j % 2 * 2 + j // 2)),
    )(low, high, got)
    mixed = call(
        functools.partial(attention_kernel, 256),
        pltpu.HBM((ctx * tokens, HEAD), bf16),
        4 * ctx * tokens * ctx * tokens * HEAD,
        2 * MB,
        name="attention",
        in_specs=[whole] * HEADS,
        out_specs=remote,
        scratch_shapes=[
            pltpu.VMEM((ctx * tokens, 3 * HEAD), bf16),
            pltpu.VMEM((ctx * tokens, HEAD), bf16),
            pltpu.SemaphoreType.DMA((ctx * tokens // 256,)),
        ],
    )(*shift_all(qkv))
    context = exchange(mixed.reshape(ctx, tokens, HEAD), "ctx")
    context = call(
        join_kernel, shape((tokens, HEADS * HEAD), bf16), 0, MB // 2, name="join"
    )(context)
    return (context[None], table_grad)


def solution(mesh):
    return jax.shard_map(
        shards,
        mesh=mesh,
        in_specs=(
            P("table", "ctx", None),
            P("table", "ctx"),
            P(("table", "ctx"), None),
            P("table", "ctx", None),
            P(),
            P(),
        ),
        out_specs=(P("table", "ctx", None), P(("table", "ctx"), None)),
        check_vma=False,
    )
```
